32 devices in a mesh: groups: 2 (over y), cube: 4 (over z), row: 2 (over x), pair: 2 (over core).
Axes of the slice: x: 2, y: 2, z: 4, core: 2. Of those that a mesh axis runs over, the one named last changes fastest.
Arguments:
- ligand: float32 [2, 64, 32, 1024], P('pair', ('groups', 'cube', 'row')), parts along dimension 1, may hold values from 0.05 to 3
- density: int32 [64, 32, 1024], P(('groups', 'cube', 'row')), parts along dimension 0, may hold values from 0 to 7
- counts: int32 [16], P(('groups', 'cube', 'row')), parts along dimension 0, may hold values from 1 to 4, as said below
- neighbours: int32 [64, 6], P(('groups', 'cube', 'row')), parts along dimension 0, may hold values from -1 to 31, as said below
- diffusion: float32 [2], replicated, may hold values from 0.04 to 0.14
- uptake: float32 [2], replicated, may hold values from 0.03 to 0.18
Outputs:
- ligand_out: float32 [2, 64, 32, 1024], P('pair', ('groups', 'cube', 'row')), parts along dimension 1
The draws below stay inside these ranges and needn't reach their ends.
There are 2 independent parts, one for each index of `groups`. The reference program is written for one: setup_inputs(seed, part) draws one part's arguments, and reference() takes and returns one part's arrays. A program takes and returns all parts, laid end to end along the dimension named above; an argument that names none is the same for every part. Nothing has to cross between parts.
Inputs may be any that keep to these rules, and one draw needn't show every extreme that they name: `counts`: the number of occupied tiles of each block of 4 slots; they fill the first slots of their block; some block is full and some block holds 1. Block b = layer * 2 + band holds tile slots b * 4 to (b + 1) * 4 - 1; an entry is -1 for an empty slot, for a face on the volume's boundary and for an unoccupied place; x neighbours lie in the same block, a -y neighbour in block b or b - 1, a +y neighbour in block b or b + 1, a -z neighbour in block b - 2, a +z neighbour in block b + 2; if tile u names v across a face, v names u across the opposite face.
All inputs are finite; a program needn't handle non-finite values.
Results may differ from the reference program's by a relative error of at most 0.00007.
Values sent between devices are 32-bit elements; how exact they have to be, the bound alone decides.
A program may use at most 64 MiB of HBM per device.

```python
import math
import jax
import jax.numpy as jnp

EX = 32
EY = 32
EZ = 32
TXN = 12
TYB = 3
SLOTS = 4
STEPS = 4
LAYERS = 4
BANDS = 2
TILES = 32


def shuffle_places(key):
    return jax.random.permutation(key, TXN * TYB)


def tissue_layout(key):
    blocks = LAYERS * BANDS
    key = jax.random.fold_in(key, 4711)
    k_count, k_full, k_thin, k_perm = jax.random.split(key, 4)
    occupied = jax.random.randint(k_count, (blocks,), SLOTS // 4, SLOTS + 1)
    full_block = jax.random.randint(k_full, (), 0, blocks)
    thin_block = (full_block + 1 + jax.random.randint(k_thin, (), 0, blocks - 1)) % blocks
    order = jnp.arange(blocks, dtype=jnp.int32)
    occupied = jnp.where(order == full_block, SLOTS, jnp.where(order == thin_block, SLOTS // 4, occupied))
    layouts = jax.vmap(shuffle_places)(jax.random.split(k_perm, blocks)).astype(jnp.int32)
    rank = jnp.argsort(layouts, axis=1).astype(jnp.int32)
    slot_at = jnp.where(rank < occupied[:, None], rank, -1)
    place = layouts[:, :SLOTS]
    column_x = place // TYB
    column_y = place % TYB
    blk = jnp.broadcast_to(order[:, None], place.shape)
    layer = blk // BANDS
    band = blk % BANDS

    def locate(target_block, target_place, allowed):
        safe_block = jnp.clip(target_block, 0, blocks - 1)
        safe_place = jnp.clip(target_place, 0, TXN * TYB - 1)
        found = slot_at[safe_block, safe_place]
        good = allowed & (found >= 0)
        return jnp.where(good, safe_block * SLOTS + found, -1)
    minus_x = locate(blk, place - TYB, column_x > 0)
    plus_x = locate(blk, place + TYB, column_x < TXN - 1)
    inside_low = column_y > 0
    minus_y = locate(jnp.where(inside_low, blk, blk - 1), jnp.where(inside_low, place - 1, place + TYB - 1), inside_low | (band > 0))
    inside_high = column_y < TYB - 1
    plus_y = locate(jnp.where(inside_high, blk, blk + 1), jnp.where(inside_high, place + 1, place - (TYB - 1)), inside_high | (band < BANDS - 1))
    minus_z = locate(blk - BANDS, place, layer > 0)
    plus_z = locate(blk + BANDS, place, layer < LAYERS - 1)
    table = jnp.stack([minus_x, plus_x, minus_y, plus_y, minus_z, plus_z], -1)
    live = jnp.arange(SLOTS, dtype=jnp.int32)[None, :] < occupied[:, None]
    table = jnp.where(live[:, :, None], table, -1).reshape(blocks * SLOTS, 6)
    return (occupied.astype(jnp.int32), table.astype(jnp.int32))


def draw_counts(key, part):
    return tissue_layout(key)[0]


def draw_neighbours(key, part):
    return tissue_layout(key)[1]


def set_ends(result, rng, low, high):
    longest = result.shape.index(max(result.shape))
    spots = []
    for shift in (0, 1):
        where = [jax.random.randint(jax.random.fold_in(rng, axis), (), 0, length) for axis, length in enumerate(result.shape)]
        where[longest] = (where[longest] + shift) % result.shape[longest]
        spots.append(tuple(where))
    return result.at[spots[0]].set(low).at[spots[1]].set(high)


def block_levels(key, extent, cuts, low, top_value):
    gain = 1.0
    for axis_at, blocks in cuts:
        heights = jax.random.uniform(jax.random.fold_in(jax.random.fold_in(key, 6), axis_at), (blocks,), jnp.float32, low / len(cuts), top_value / len(cuts))
        gain = gain * jnp.repeat(jnp.exp(heights), extent[axis_at] // blocks).reshape((-1,) + (1,) * (len(extent) - 1 - axis_at))
    return gain


def setup_inputs(seed: int = 0, part: int = 0) -> dict:
    arg_keys = jax.random.split(jax.random.key(seed), 7)
    own_keys = jax.random.split(jax.random.fold_in(arg_keys[6], part), 7)
    return {
        "ligand": jnp.clip(jnp.exp(math.log(3.0) - 4.0943445 * jax.random.uniform(own_keys[0], (2, TILES, EZ, EX * EY), jnp.float32) ** block_levels(own_keys[0], (2, TILES, EZ, EX * EY), ((0, 2), (1, 8)), -0.2, 0.2)), 0.05, 3.0),
        "density": set_ends(jax.random.randint(own_keys[1], (TILES, EZ, EX * EY), 0, 8), jax.random.fold_in(own_keys[1], 1), 0, 7).astype(jnp.int32),
        "counts": draw_counts(jax.random.fold_in(jax.random.fold_in(arg_keys[6], part), 71), part),
        "neighbours": draw_neighbours(jax.random.fold_in(jax.random.fold_in(arg_keys[6], part), 71), part),
        "diffusion": jnp.clip(jax.random.uniform(arg_keys[4], (2,), jnp.float32, 0.04, 0.14), 0.04, 0.14),
        "uptake": jnp.clip(jnp.exp(jax.random.uniform(arg_keys[5], (2,), jnp.float32, math.log(0.03), math.log(0.18))), 0.03, 0.18),
    }


def ghost_cells(face, column, neighbours):
    index = neighbours[:, column]
    picked = jnp.take(face, jnp.clip(index, 0, TILES - 1), axis=1)
    okay = (index >= 0).reshape((1, -1, 1, 1, 1))
    return jnp.where(okay, picked, jnp.float32(0.0))


def neighbour_sum(field, neighbours):
    x_minus = jnp.concatenate([ghost_cells(field[:, :, :, -1:, :], 0, neighbours), field[:, :, :, :-1, :]], 3)
    x_plus = jnp.concatenate([field[:, :, :, 1:, :], ghost_cells(field[:, :, :, :1, :], 1, neighbours)], 3)
    y_minus = jnp.concatenate([ghost_cells(field[:, :, :, :, -1:], 2, neighbours), field[:, :, :, :, :-1]], 4)
    y_plus = jnp.concatenate([field[:, :, :, :, 1:], ghost_cells(field[:, :, :, :, :1], 3, neighbours)], 4)
    z_minus = jnp.concatenate([ghost_cells(field[:, :, -1:], 4, neighbours), field[:, :, :-1]], 2)
    z_plus = jnp.concatenate([field[:, :, 1:], ghost_cells(field[:, :, :1], 5, neighbours)], 2)
    return x_minus + x_plus + y_minus + y_plus + z_minus + z_plus


def reference(ligand, density, counts, neighbours, diffusion, uptake):
    field = ligand.reshape(2, TILES, EZ, EX, EY)
    scaled = density.reshape(TILES, EZ, EX, EY).astype(jnp.float32) / 8.0
    slot_ids = jnp.arange(TILES, dtype=jnp.int32) % SLOTS
    filled = slot_ids < jnp.repeat(counts, SLOTS)
    field = jnp.where(filled.reshape(1, -1, 1, 1, 1), field, jnp.float32(0.0))
    rate = diffusion.reshape(2, 1, 1, 1, 1)
    rate_up = uptake.reshape(2, 1, 1, 1, 1)
    for step in range(STEPS):
        total = field[0] + field[1]
        nsum = neighbour_sum(field, neighbours)
        field = field + rate * (nsum - 6.0 * field) - rate_up * scaled[None] * field / (1.0 + total)[None]
    return field.reshape(2, TILES, EZ, EX * EY)
```

```python
import functools

import jax
import jax.numpy as jnp
from jax import lax
from jax.experimental import pallas as pl
from jax.experimental.pallas import tpu as pltpu
from jax.sharding import PartitionSpec as P

EY = 32
STEPS = 4
LANES = 128
ROWS = 8
MESH = pl.DeviceIdType.MESH


def kernel(
    layers, bands, slots, half, cells,
    nbr_in, counts_in, diffusion_in, uptake_in, ligand, density, out,
    field, dens, stage, y_high, y_low, y_minus, y_plus, z_low, z_high, z_minus, z_plus,
    extra, y_first, y_here, z_first_low, z_first_high, nbr, counts, diffusion, uptake,
    first_send, first_recv,
    load_sem, small_sem, swap_send, swap_recv, face_send, face_recv, out_send, out_recv,
):
    core = lax.axis_index("pair")
    layer = lax.axis_index("cube")
    band = lax.axis_index("row")
    block = layer * bands + band
    other = 1 - core
    part = lax.rem(core + band, 2)
    rest = 1 - part
    low_core = lax.rem(band, 2)
    high_core = 1 - low_core
    columns = cells // LANES
    has_minus = band > 0
    has_plus = band < bands - 1
    far_layer = jnp.where(part == 0, layer - 1, layer + 1)
    has_far = jnp.logical_and(far_layer >= 0, far_layer < layers)
    partner_id = {"pair": other}
    far_id = {"cube": far_layer, "pair": other}
    minus_id = {"row": band - 1, "pair": other}
    plus_id = {"row": band + 1, "pair": other}

    own_rows = pl.ds(pl.multiple_of(part * half, half), half)
    other_rows = pl.ds(pl.multiple_of(rest * half, half), half)
    loads = [
        pltpu.make_async_copy(ligand.at[0, :, own_rows, :], field.at[0, core], load_sem.at[0]),
        pltpu.make_async_copy(ligand.at[0, :, other_rows, :], extra, load_sem.at[2]),
        pltpu.make_async_copy(density.at[:, own_rows, :], dens, load_sem.at[1]),
    ]
    smalls = [
        pltpu.make_async_copy(source, target, small_sem.at[k])
        for k, (source, target) in enumerate(
            [(nbr_in, nbr), (counts_in, counts), (diffusion_in, diffusion), (uptake_in, uptake)]
        )
    ]
    for load in loads + smalls:
        load.start()

    barrier = pltpu.get_barrier_semaphore()
    has_down = layer > 0
    has_up = layer < layers - 1
    always = layer >= 0
    greeted = [
        (always, partner_id),
        (has_far, far_id),
        (has_down, {"cube": layer - 1}),
        (has_up, {"cube": layer + 1}),
        (has_minus, minus_id),
        (has_plus, plus_id),
        (has_minus, {"row": band - 1}),
        (has_plus, {"row": band + 1}),
    ]
    peers = jnp.int32(0)
    for wanted, device in greeted:
        pl.when(wanted)(
            functools.partial(
                pl.semaphore_signal, barrier, inc=1, device_id=device, device_id_type=MESH
            )
        )
        peers = peers + wanted.astype(jnp.int32)
    pl.semaphore_wait(barrier, peers)

    swap = pltpu.make_async_remote_copy(
        src_ref=ligand.at[0, :, other_rows, :], dst_ref=field.at[0, core],
        send_sem=swap_send, recv_sem=swap_recv, device_id=partner_id, device_id_type=MESH,
    )
    swap_in = pltpu.make_async_remote_copy(
        src_ref=ligand.at[0, :, other_rows, :], dst_ref=field.at[0, other],
        send_sem=swap_send, recv_sem=swap_recv, device_id=partner_id, device_id_type=MESH,
    )
    swap.start()

    def remote(source, target, step, k, device):
        return pltpu.make_async_remote_copy(
            src_ref=source.at[step], dst_ref=target[step],
            send_sem=face_send.at[step, k], recv_sem=face_recv.at[step, k],
            device_id=device, device_id_type=MESH,
        )

    def messages(step):
        first, last = part == 0, part == 1
        up_far = remote(z_high, z_minus, step, 0, far_id)
        up_near = remote(z_high, z_minus, step, 0, partner_id)
        down_far = remote(z_low, z_plus, step, 1, far_id)
        down_near = remote(z_low, z_plus, step, 1, partner_id)
        to_plus = remote(y_high, y_minus, step, 2, plus_id)
        to_minus = remote(y_low, y_plus, step, 3, minus_id)
        both = jnp.logical_and
        sends = [
            (has_plus, to_plus), (has_minus, to_minus),
            (both(last, has_far), up_far), (both(first, has_far), down_far),
            (first, up_near), (last, down_near),
        ]
        receives = [
            (jnp.logical_or(last, has_far), up_near), (jnp.logical_or(first, has_far), down_near),
            (has_minus, to_plus), (has_plus, to_minus),
        ]
        return sends, receives

    def first_copy(source, target, k, at, device):
        return pltpu.make_async_remote_copy(
            src_ref=source, dst_ref=target.at[core],
            send_sem=first_send.at[k], recv_sem=first_recv.at[at, core],
            device_id=device, device_id_type=MESH,
        )

    def first_sends():
        return [
            (part == 0, first_copy(z_first_high.at[0], z_minus[0], 0, 0, partner_id)),
            (part == 1, first_copy(z_first_low.at[1], z_plus[0], 1, 1, partner_id)),
            (has_down, first_copy(
                z_first_low.at[0], z_plus[0], 2, 1, {"cube": layer - 1, "pair": high_core})),
            (has_up, first_copy(
                z_first_high.at[1], z_minus[0], 3, 0, {"cube": layer + 1, "pair": low_core})),
        ] + [
            (has_plus, first_copy(
                y_first.at[h], y_minus[0], 4 + h, 2, {"row": band + 1, "pair": lax.rem(band + 1 + h, 2)}))
            for h in range(2)
        ] + [
            (has_minus, first_copy(
                y_first.at[h], y_plus[0], 6 + h, 3, {"row": band - 1, "pair": lax.rem(band + 1 + h, 2)}))
            for h in range(2)
        ]

    def arrived(target, at, species):
        pltpu.make_async_remote_copy(
            src_ref=target.at[species], dst_ref=target.at[species],
            send_sem=first_send.at[0], recv_sem=first_recv.at[at, species],
            device_id=partner_id, device_id_type=MESH,
        ).wait_recv()

    def wait_first():
        both, either = jnp.logical_and, jnp.logical_or
        for species in range(2):
            across = core == 1 - species
            minus = either(both(part == 0, has_down), both(part == 1, across))
            plus = either(both(part == 1, has_up), both(part == 0, across))
            pl.when(minus)(functools.partial(arrived, z_minus[0], 0, species))
            pl.when(plus)(functools.partial(arrived, z_plus[0], 1, species))
            pl.when(has_minus)(functools.partial(arrived, y_minus[0], 2, species))
            pl.when(has_plus)(functools.partial(arrived, y_plus[0], 3, species))

    def send_faces(step):
        for wanted, copy in messages(step)[0]:
            pl.when(wanted)(copy.start)

    def wait_faces(step):
        for wanted, copy in messages(step)[1]:
            pl.when(wanted)(copy.wait_recv)

    def wait_sent(step):
        for wanted, copy in messages(step)[0]:
            pl.when(wanted)(copy.wait_send)

    lane = lax.broadcasted_iota(jnp.int32, (ROWS, LANES), 1)
    pair_of = lax.rem(lane + 1, EY) // 2
    even = lax.rem(lane, 2) == 0
    wide = lax.broadcasted_iota(jnp.int32, (half, LANES), 1)
    at_low = lax.rem(wide, EY) == 0
    at_high = lax.rem(wide, EY) == EY - 1
    at_edge = jnp.logical_or(at_low, at_high)
    below_32 = wide < EY
    above_96 = wide >= LANES - EY

    def roll(value, shift):
        shift = shift % LANES
        return value if shift == 0 else pltpu.roll(value, shift, axis=1)

    pieces = [(zv, j) for zv in range(half // ROWS) for j in range(columns)]

    def pack(parts):
        total = None
        for m, (zv, j) in enumerate(pieces):
            piece = roll(parts[j][zv * ROWS : (zv + 1) * ROWS], 2 * m)
            total = piece if total is None else jnp.where(pair_of == m, piece, total)
        return total

    def put_faces(step, tile, both):
        packed = []
        for species in range(2):
            parts = both[species]
            packed.append(pack(parts))
            for j in range(columns):
                at = slice(j * LANES, (j + 1) * LANES)
                z_low[step, species, tile, :, at] = parts[j][:1]
                z_high[step, species, tile, :, at] = parts[j][half - 1 :]
        second = roll(packed[1], 1)
        y_low[step, tile] = jnp.where(even, packed[0], second)
        y_high[step, tile] = jnp.where(even, second, packed[0])

    def columns_of(value):
        return [value[:, j * LANES : (j + 1) * LANES] for j in range(columns)]

    def first_faces(tile, carry):
        for h, value in ((part, field[0, core, tile]), (rest, extra[tile])):
            packed = pack(columns_of(value))
            y_first[h, tile] = packed
            z_first_low[h, tile] = value[:1]
            z_first_high[h, tile] = value[half - 1 :]
            if h is part:
                y_here[core, tile] = packed
        return carry

    def other_faces(tile, carry):
        y_here[other, tile] = pack(columns_of(field[0, other, tile]))
        return carry

    def own_planes():
        @pl.when(part == 0)
        def _():
            z_plus[0][core] = z_first_low[1]

        @pl.when(part == 1)
        def _():
            z_minus[0][core] = z_first_high[0]

    zero = jnp.float32(0.0)
    row = lax.broadcasted_iota(jnp.int32, (half, LANES), 0)

    def entry(tile, k):
        value = nbr[tile, k]
        safe = jnp.maximum(value, 0)
        return value >= 0, lax.rem(safe, slots), safe // slots == block

    def inner(step, tile):
        now, later = step % 2, (step + 1) % 2
        filled = tile < counts[0]
        left_ok, left, _ = entry(tile, 0)
        right_ok, right, _ = entry(tile, 1)
        fields = []
        for species in range(2):
            parts = columns_of(field[now, species, tile])
            if step == 0:
                parts = [jnp.where(filled, part, zero) for part in parts]
            fields.append(parts)
        amount = columns_of(dens[tile])
        share = [
            amount[j].astype(jnp.float32) / (1.0 + fields[0][j] + fields[1][j])
            for j in range(columns)
        ]
        blank = jnp.zeros((1, LANES), jnp.float32)
        for species in range(2):
            parts = fields[species]
            rate = diffusion[species]
            keep = 1.0 - 6.0 * rate
            taken = uptake[species] * 0.125
            ghost_left = roll(field[now, species, left, :, cells - LANES :], EY)
            ghost_right = roll(field[now, species, right, :, :LANES], -EY)
            forward = [jnp.where(left_ok, ghost_left, zero)] + [roll(part, EY) for part in parts]
            backward = [roll(part, -EY) for part in parts] + [jnp.where(right_ok, ghost_right, zero)]
            for j in range(columns):
                part = parts[j]
                value = jnp.where(below_32, forward[j], forward[j + 1])
                value = value + jnp.where(above_96, backward[j + 1], backward[j])
                value = value + jnp.where(at_low, zero, roll(part, 1))
                value = value + jnp.where(at_high, zero, roll(part, -1))
                value = value + jnp.concatenate([blank, part[: half - 1]], axis=0)
                value = value + jnp.concatenate([part[1:], blank], axis=0)
                at = slice(j * LANES, (j + 1) * LANES)
                field[later, species, tile, :, at] = (
                    part * (keep - taken * share[j]) + rate * value
                )

    def outer(step, tile):
        later = (step + 1) % 2
        filled = tile < counts[0]
        front_ok, front, front_here = entry(tile, 2)
        back_ok, back, back_here = entry(tile, 3)
        lower_ok, lower, _ = entry(tile, 4)
        upper_ok, upper, _ = entry(tile, 5)
        first = part == 0
        lower = jnp.where(first, lower, tile)
        lower_ok = jnp.where(first, lower_ok, filled)
        upper = jnp.where(first, tile, upper)
        upper_ok = jnp.where(first, filled, upper_ok)
        result = []
        for species in range(2):
            rate = diffusion[species]
            if step == 0:
                shift = 0
                from_front = jnp.where(front_here, y_here[species, front], y_minus[0][species, front])
                from_back = jnp.where(back_here, y_here[species, back], y_plus[0][species, back])
            else:
                shift = species
                from_front = jnp.where(front_here, y_high[step, front], y_minus[step][front])
                from_back = jnp.where(back_here, y_low[step, back], y_plus[step][back])
            from_front = jnp.where(front_ok, from_front, zero)
            from_back = jnp.where(back_ok, from_back, zero)
            ghost_y = rate * jnp.where(
                even, roll(from_front, 1 - EY - shift), roll(from_back, EY - 1 - shift)
            )
            below = rate * jnp.where(lower_ok, z_minus[step][species, lower], zero)
            above = rate * jnp.where(upper_ok, z_plus[step][species, upper], zero)
            values = []
            for j in range(columns):
                at = slice(j * LANES, (j + 1) * LANES)
                edge = jnp.concatenate(
                    [roll(ghost_y, -2 * (zv * columns + j)) for zv in range(half // ROWS)], axis=0
                )
                value = field[later, species, tile, :, at] + jnp.where(at_edge, edge, zero)
                value = value + jnp.where(row == 0, below[:, at], zero)
                value = value + jnp.where(row == half - 1, above[:, at], zero)
                values.append(value)
            result.append(values)
        return result

    def inner_step(step):
        def body(tile, carry):
            inner(step, tile)
            return carry

        lax.fori_loop(0, slots, body, 0)

    def outer_step(step):
        later = (step + 1) % 2

        def body(tile, carry):
            result = outer(step, tile)
            for species in range(2):
                for j in range(columns):
                    at = slice(j * LANES, (j + 1) * LANES)
                    field[later, species, tile, :, at] = result[species][j]
            put_faces(step + 1, tile, result)
            return carry

        lax.fori_loop(0, slots, body, 0, unroll=True)

    def give(tile):
        return pltpu.make_async_remote_copy(
            src_ref=stage.at[tile], dst_ref=out.at[0, tile, own_rows, :],
            send_sem=out_send.at[tile], recv_sem=out_recv.at[tile],
            device_id=partner_id, device_id_type=MESH,
        )

    def take(tile):
        return pltpu.make_async_remote_copy(
            src_ref=stage.at[tile], dst_ref=out.at[0, tile, other_rows, :],
            send_sem=out_send.at[tile], recv_sem=out_recv.at[tile],
            device_id=partner_id, device_id_type=MESH,
        )

    for load in smalls:
        load.wait()
    loads[0].wait()
    loads[1].wait()
    lax.fori_loop(0, slots, first_faces, 0, unroll=True)
    for wanted, copy in first_sends():
        pl.when(wanted)(copy.start)
    own_planes()
    loads[2].wait()
    swap_in.wait_recv()
    lax.fori_loop(0, slots, other_faces, 0, unroll=True)
    for step in range(STEPS):
        inner_step(step)
        if step == 0:
            wait_first()
        else:
            wait_faces(step)
        if step < STEPS - 1:
            outer_step(step)
            send_faces(step + 1)

    def last_body(tile, carry):
        result = outer(STEPS - 1, tile)
        for j in range(columns):
            at = slice(j * LANES, (j + 1) * LANES)
            stage[tile, :, at] = jnp.where(core == 0, result[1][j], result[0][j])
        give(tile).start()
        for j in range(columns):
            at = slice(j * LANES, (j + 1) * LANES)
            out[0, tile, own_rows, at] = jnp.where(core == 0, result[0][j], result[1][j])
        return carry

    lax.fori_loop(0, slots, last_body, 0, unroll=True)
    swap.wait_send()
    for wanted, copy in first_sends():
        pl.when(wanted)(copy.wait_send)
    for step in range(1, STEPS):
        wait_sent(step)
    for tile in range(slots):
        give(tile).wait_send()
        take(tile).wait_recv()


def per_device(layers, bands, ligand, density, counts, neighbours, diffusion, uptake):
    _, slots, depth, cells = ligand.shape
    half = depth // 2
    faces = (slots, ROWS, LANES)
    planes = (2, slots, 1, cells)
    away = pl.BlockSpec(memory_space=pltpu.HBM)
    return pl.pallas_call(
        functools.partial(kernel, layers, bands, slots, half, cells),
        out_shape=jax.ShapeDtypeStruct(ligand.shape, jnp.float32),
        in_specs=[away] * 6,
        out_specs=pl.BlockSpec(memory_space=pltpu.VMEM),
        scratch_shapes=[
            pltpu.VMEM((2, 2, slots, half, cells), jnp.float32),
            pltpu.VMEM((slots, half, cells), jnp.int32),
            pltpu.VMEM((slots, half, cells), jnp.float32),
            pltpu.VMEM((STEPS,) + faces, jnp.float32),
            pltpu.VMEM((STEPS,) + faces, jnp.float32),
            [pltpu.VMEM((2,) + faces, jnp.float32)] + [pltpu.VMEM(faces, jnp.float32)] * (STEPS - 1),
            [pltpu.VMEM((2,) + faces, jnp.float32)] + [pltpu.VMEM(faces, jnp.float32)] * (STEPS - 1),
            pltpu.VMEM((STEPS,) + planes, jnp.float32),
            pltpu.VMEM((STEPS,) + planes, jnp.float32),
            [pltpu.VMEM(planes, jnp.float32)] * STEPS,
            [pltpu.VMEM(planes, jnp.float32)] * STEPS,
            pltpu.VMEM((slots, half, cells), jnp.float32),
            pltpu.VMEM((2,) + faces, jnp.float32),
            pltpu.VMEM((2,) + faces, jnp.float32),
            pltpu.VMEM(planes, jnp.float32),
            pltpu.VMEM(planes, jnp.float32),
            pltpu.SMEM((slots, 6), jnp.int32),
            pltpu.SMEM((1,), jnp.int32),
            pltpu.SMEM((2,), jnp.float32),
            pltpu.SMEM((2,), jnp.float32),
            pltpu.SemaphoreType.DMA((8,)),
            pltpu.SemaphoreType.DMA((4, 2)),
            pltpu.SemaphoreType.DMA((3,)),
            pltpu.SemaphoreType.DMA((4,)),
            pltpu.SemaphoreType.DMA,
            pltpu.SemaphoreType.DMA,
            pltpu.SemaphoreType.DMA((STEPS, 4)),
            pltpu.SemaphoreType.DMA((STEPS, 4)),
            pltpu.SemaphoreType.DMA((slots,)),
            pltpu.SemaphoreType.DMA((slots,)),
        ],
        compiler_params=pltpu.CompilerParams(
            collective_id=0, has_side_effects=True, vmem_limit_bytes=53 * 1024 * 1024
        ),
    )(neighbours, counts, diffusion, uptake, ligand, density)


def solution(mesh):
    in_specs = (
        P("pair", ("groups", "cube", "row"), None, None),
        P(("groups", "cube", "row"), None, None),
        P(("groups", "cube", "row")),
        P(("groups", "cube", "row"), None),
        P(),
        P(),
    )
    out_specs = P("pair", ("groups", "cube", "row"), None, None)
    return jax.shard_map(
        functools.partial(per_device, mesh.shape["cube"], mesh.shape["row"]),
        mesh=mesh, in_specs=in_specs, out_specs=out_specs, check_vma=False,
    )
```

```python
import functools

import jax
import jax.numpy as jnp
from jax import lax
from jax.experimental import pallas as pl
from jax.experimental.pallas import tpu as pltpu
from jax.sharding import PartitionSpec as P

EY = 32
STEPS = 4
LANES = 128
ROWS = 8
MESH = pl.DeviceIdType.MESH


def kernel(
    layers, bands, slots, half, cells,
    nbr_in, counts_in, diffusion_in, uptake_in, ligand, density, out,
    field, dens, y_low, y_high, y_minus, y_plus, z_low, z_high, z_minus, z_plus,
    extra, y_first, y_here, z_first_low, z_first_high,
    y_part, y_ghost, z_ghost_low, z_ghost_high,
    y_last, y_last_here, y_last_minus, y_last_plus, z_last_minus, z_last_plus, z_near,
    nbr, counts, diffusion, uptake,
    first_send, first_recv, load_sem, small_sem, swap_send, swap_recv, face_send, face_recv,
    last_send, last_recv, out_send, out_recv,
):
    core = lax.axis_index("pair")
    layer = lax.axis_index("cube")
    band = lax.axis_index("row")
    block = layer * bands + band
    other = 1 - core
    part = lax.rem(core + band, 2)
    rest = 1 - part
    low_core = lax.rem(band, 2)
    high_core = 1 - low_core
    columns = cells // LANES
    has_minus = band > 0
    has_plus = band < bands - 1
    far_layer = jnp.where(part == 0, layer - 1, layer + 1)
    has_far = jnp.logical_and(far_layer >= 0, far_layer < layers)
    partner_id = {"pair": other}
    far_id = {"cube": far_layer, "pair": other}
    minus_id = {"row": band - 1, "pair": other}
    plus_id = {"row": band + 1, "pair": other}

    own_rows = pl.ds(pl.multiple_of(part * half, half), half)
    other_rows = pl.ds(pl.multiple_of(rest * half, half), half)
    loads = [
        pltpu.make_async_copy(ligand.at[0, :, own_rows, :], field.at[0, core], load_sem.at[0]),
        pltpu.make_async_copy(ligand.at[0, :, other_rows, :], extra, load_sem.at[2]),
        pltpu.make_async_copy(density.at[:, own_rows, :], dens, load_sem.at[1]),
    ]
    smalls = [
        pltpu.make_async_copy(source, target, small_sem.at[k])
        for k, (source, target) in enumerate(
            [(nbr_in, nbr), (counts_in, counts), (diffusion_in, diffusion), (uptake_in, uptake)]
        )
    ]
    for load in loads + smalls:
        load.start()

    barrier = pltpu.get_barrier_semaphore()
    has_down = layer > 0
    has_up = layer < layers - 1
    always = layer >= 0
    greeted = [
        (always, partner_id),
        (has_far, far_id),
        (has_down, {"cube": layer - 1}),
        (has_up, {"cube": layer + 1}),
        (has_minus, minus_id),
        (has_plus, plus_id),
        (has_minus, {"row": band - 1}),
        (has_plus, {"row": band + 1}),
    ]
    peers = jnp.int32(0)
    for wanted, device in greeted:
        pl.when(wanted)(
            functools.partial(
                pl.semaphore_signal, barrier, inc=1, device_id=device, device_id_type=MESH
            )
        )
        peers = peers + wanted.astype(jnp.int32)

    swap = pltpu.make_async_remote_copy(
        src_ref=ligand.at[0, :, other_rows, :], dst_ref=field.at[0, core],
        send_sem=swap_send, recv_sem=swap_recv, device_id=partner_id, device_id_type=MESH,
    )
    swap_in = pltpu.make_async_remote_copy(
        src_ref=ligand.at[0, :, other_rows, :], dst_ref=field.at[0, other],
        send_sem=swap_send, recv_sem=swap_recv, device_id=partner_id, device_id_type=MESH,
    )

    def remote(source, target, step, k, device):
        return pltpu.make_async_remote_copy(
            src_ref=source.at[step], dst_ref=target[step],
            send_sem=face_send.at[step, k], recv_sem=face_recv.at[step, k],
            device_id=device, device_id_type=MESH,
        )

    def messages(step):
        first, last = part == 0, part == 1
        up_far = remote(z_high, z_minus, step, 0, far_id)
        up_near = remote(z_high, z_minus, step, 0, partner_id)
        down_far = remote(z_low, z_plus, step, 1, far_id)
        down_near = remote(z_low, z_plus, step, 1, partner_id)
        to_plus = remote(y_high, y_minus, step, 2, plus_id)
        to_minus = remote(y_low, y_plus, step, 3, minus_id)
        both = jnp.logical_and
        sends = [
            (has_plus, to_plus), (has_minus, to_minus),
            (both(last, has_far), up_far), (both(first, has_far), down_far),
            (first, up_near), (last, down_near),
        ]
        receives = [
            (jnp.logical_or(last, has_far), up_near), (jnp.logical_or(first, has_far), down_near),
            (has_minus, to_plus), (has_plus, to_minus),
        ]
        return sends, receives

    def first_copy(source, target, k, at, device):
        return pltpu.make_async_remote_copy(
            src_ref=source, dst_ref=target.at[core],
            send_sem=first_send.at[k], recv_sem=first_recv.at[at, core],
            device_id=device, device_id_type=MESH,
        )

    def first_sends():
        return [
            (part == 0, first_copy(z_first_high.at[0], z_minus[0], 0, 0, partner_id)),
            (part == 1, first_copy(z_first_low.at[1], z_plus[0], 1, 1, partner_id)),
            (has_down, first_copy(
                z_first_low.at[0], z_plus[0], 2, 1, {"cube": layer - 1, "pair": high_core})),
            (has_up, first_copy(
                z_first_high.at[1], z_minus[0], 3, 0, {"cube": layer + 1, "pair": low_core})),
        ] + [
            (has_plus, first_copy(
                y_first.at[h], y_minus[0], 4 + h, 2, {"row": band + 1, "pair": lax.rem(band + 1 + h, 2)}))
            for h in range(2)
        ] + [
            (has_minus, first_copy(
                y_first.at[h], y_plus[0], 6 + h, 3, {"row": band - 1, "pair": lax.rem(band + 1 + h, 2)}))
            for h in range(2)
        ]

    def arrived(target, at, species):
        pltpu.make_async_remote_copy(
            src_ref=target.at[species], dst_ref=target.at[species],
            send_sem=first_send.at[0], recv_sem=first_recv.at[at, species],
            device_id=partner_id, device_id_type=MESH,
        ).wait_recv()

    def wait_first():
        both, either = jnp.logical_and, jnp.logical_or
        for species in range(2):
            across = core == 1 - species
            minus = either(both(part == 0, has_down), both(part == 1, across))
            plus = either(both(part == 1, has_up), both(part == 0, across))
            pl.when(minus)(functools.partial(arrived, z_minus[0], 0, species))
            pl.when(plus)(functools.partial(arrived, z_plus[0], 1, species))
            pl.when(has_minus)(functools.partial(arrived, y_minus[0], 2, species))
            pl.when(has_plus)(functools.partial(arrived, y_plus[0], 3, species))

    def send_faces(step):
        for wanted, copy in messages(step)[0]:
            pl.when(wanted)(copy.start)

    def wait_faces(step):
        for wanted, copy in messages(step)[1]:
            pl.when(wanted)(copy.wait_recv)

    def wait_sent(step):
        for wanted, copy in messages(step)[0]:
            pl.when(wanted)(copy.wait_send)

    lane = lax.broadcasted_iota(jnp.int32, (ROWS, LANES), 1)
    pair_of = lax.rem(lane + 1, EY) // 2
    even = lax.rem(lane, 2) == 0
    wide = lax.broadcasted_iota(jnp.int32, (half, LANES), 1)
    at_low = lax.rem(wide, EY) == 0
    at_high = lax.rem(wide, EY) == EY - 1
    at_edge = jnp.logical_or(at_low, at_high)
    below_32 = wide < EY
    above_96 = wide >= LANES - EY

    def roll(value, shift):
        shift = shift % LANES
        return value if shift == 0 else pltpu.roll(value, shift, axis=1)

    pieces = [(zv, j) for zv in range(half // ROWS) for j in range(columns)]

    def pack(parts):
        total = None
        for m, (zv, j) in enumerate(pieces):
            piece = roll(parts[j][zv * ROWS : (zv + 1) * ROWS], 2 * m)
            total = piece if total is None else jnp.where(pair_of == m, piece, total)
        return total

    def columns_of(value):
        return [value[:, j * LANES : (j + 1) * LANES] for j in range(columns)]

    def first_faces():
        for tile in range(slots):
            for h, value in ((part, field[0, core, tile]), (rest, extra[tile])):
                packed = pack(columns_of(value))
                y_first[h, tile] = packed
                z_first_low[h, tile : tile + 1, :] = value[:1]
                z_first_high[h, tile : tile + 1, :] = value[half - 1 :]
                if h is part:
                    y_here[core, tile] = packed

    def other_faces(tile, carry):
        y_here[other, tile] = pack(columns_of(field[0, other, tile]))
        return carry

    def own_planes():
        @pl.when(part == 0)
        def _():
            z_plus[0][core] = z_first_low[1]

        @pl.when(part == 1)
        def _():
            z_minus[0][core] = z_first_high[0]

    zero = jnp.float32(0.0)
    row = lax.broadcasted_iota(jnp.int32, (half, LANES), 0)

    def entry(tile, k):
        value = nbr[tile, k]
        safe = jnp.maximum(value, 0)
        return value >= 0, lax.rem(safe, slots), safe // slots == block

    def inner(step, tile, keep_faces):
        now, later = step % 2, (step + 1) % 2
        filled = tile < counts[0]
        left_ok, left, _ = entry(tile, 0)
        right_ok, right, _ = entry(tile, 1)
        fields = []
        for species in range(2):
            parts = columns_of(field[now, species, tile])
            if step == 0:
                parts = [jnp.where(filled, part, zero) for part in parts]
            fields.append(parts)
        amount = columns_of(dens[tile])
        share = [
            amount[j].astype(jnp.float32) / (1.0 + fields[0][j] + fields[1][j])
            for j in range(columns)
        ]
        blank = jnp.zeros((1, LANES), jnp.float32)
        for species in range(2):
            parts = fields[species]
            rate = diffusion[species]
            keep = 1.0 - 6.0 * rate
            taken = uptake[species] * 0.125
            ghost_left = roll(field[now, species, left, :, cells - LANES :], EY)
            ghost_right = roll(field[now, species, right, :, :LANES], -EY)
            forward = [jnp.where(left_ok, ghost_left, zero)] + [roll(part, EY) for part in parts]
            backward = [roll(part, -EY) for part in parts] + [jnp.where(right_ok, ghost_right, zero)]
            values = []
            for j in range(columns):
                part = parts[j]
                value = jnp.where(below_32, forward[j], forward[j + 1])
                value = value + jnp.where(above_96, backward[j + 1], backward[j])
                value = value + jnp.where(at_low, zero, roll(part, 1))
                value = value + jnp.where(at_high, zero, roll(part, -1))
                value = value + jnp.concatenate([blank, part[: half - 1]], axis=0)
                value = value + jnp.concatenate([part[1:], blank], axis=0)
                value = part * (keep - taken * share[j]) + rate * value
                field[later, species, tile, :, j * LANES : (j + 1) * LANES] = value
                values.append(value)
            if keep_faces:
                y_part[species, tile] = pack(values)

    top = (half // ROWS - 1) * columns
    sub = lax.broadcasted_iota(jnp.int32, (ROWS, LANES), 0)
    in_low = jnp.logical_and(sub == 0, pair_of < columns)
    in_high = jnp.logical_and(sub == ROWS - 1, pair_of >= top)
    first_row = sub == 0
    last_row = sub == ROWS - 1
    row_pair = lax.rem(lax.broadcasted_iota(jnp.int32, (slots, LANES), 1) + 1, EY) // 2
    row_edge = row_pair == 0

    def pick(ok, ref, *at):
        return jnp.where(ok, ref[at], zero)

    def ghost_of(rate, from_front, from_back, shift):
        return rate * jnp.where(
            even, roll(from_front, 1 - EY - shift), roll(from_back, EY - 1 - shift)
        )

    def compact(step):
        later = (step + 1) % 2
        first = part == 0
        for tile in range(slots):
            filled = tile < counts[0]
            front_ok, front, front_here = entry(tile, 2)
            back_ok, back, back_here = entry(tile, 3)
            lower_ok, lower, _ = entry(tile, 4)
            upper_ok, upper, _ = entry(tile, 5)
            lower = jnp.where(first, lower, tile)
            lower_ok = jnp.where(first, lower_ok, filled)
            upper = jnp.where(first, tile, upper)
            upper_ok = jnp.where(first, filled, upper_ok)
            for species in range(2):
                rate = diffusion[species]
                if step == 0:
                    shift = 0
                    from_front = jnp.where(
                        front_here, y_here[species, front], y_minus[0][species, front])
                    from_back = jnp.where(
                        back_here, y_here[species, back], y_plus[0][species, back])
                else:
                    shift = species
                    from_front = jnp.where(front_here, y_high[step, front], y_minus[step][front])
                    from_back = jnp.where(back_here, y_low[step, back], y_plus[step][back])
                from_front = jnp.where(front_ok, from_front, zero)
                from_back = jnp.where(back_ok, from_back, zero)
                y_ghost[species, tile] = ghost_of(rate, from_front, from_back, shift)
                at = slice(tile, tile + 1)
                below = rate * pick(lower_ok, z_minus[step], species, pl.ds(lower, 1), slice(None))
                above = rate * pick(upper_ok, z_plus[step], species, pl.ds(upper, 1), slice(None))
                z_ghost_low[species, at, :] = below
                z_ghost_high[species, at, :] = above
                z_low[step + 1, species, at, :] = field[later, species, tile, :1, :] + below
                z_high[step + 1, species, at, :] = field[later, species, tile, half - 1 :, :] + above
        packed = []
        for species in range(2):
            ghosts = [y_ghost[species, tile] for tile in range(slots)]
            edge_low = jnp.concatenate([ghost[:1] for ghost in ghosts], axis=0)
            edge_high = jnp.concatenate([ghost[ROWS - 1 :] for ghost in ghosts], axis=0)
            pack_low = jnp.zeros((slots, LANES), jnp.float32)
            pack_high = jnp.zeros((slots, LANES), jnp.float32)
            for j in range(columns):
                at = slice(j * LANES, (j + 1) * LANES)
                low = roll(z_ghost_low[species, :, at], 2 * j)
                high = roll(z_ghost_high[species, :, at], 2 * (top + j))
                pack_low = jnp.where(row_pair == j, low, pack_low)
                pack_high = jnp.where(row_pair == top + j, high, pack_high)
                z_low[step + 1, species, :, at] += jnp.where(row_edge, roll(edge_low, -2 * j), zero)
                z_high[step + 1, species, :, at] += jnp.where(
                    row_edge, roll(edge_high, -2 * (top + j)), zero)
            packed.append([
                y_part[species, tile] + ghosts[tile]
                + jnp.where(in_low, jnp.broadcast_to(pack_low[tile : tile + 1], (ROWS, LANES)), zero)
                + jnp.where(in_high, jnp.broadcast_to(pack_high[tile : tile + 1], (ROWS, LANES)), zero)
                for tile in range(slots)
            ])
        for tile in range(slots):
            if step + 1 == STEPS - 1:
                for species in range(2):
                    y_last[species, tile] = packed[species][tile]
            else:
                second = roll(packed[1][tile], 1)
                y_low[step + 1, tile] = jnp.where(even, packed[0][tile], second)
                y_high[step + 1, tile] = jnp.where(even, second, packed[0][tile])

    def inner_step(step):
        def body(tile, carry):
            inner(step, tile, step < STEPS - 1)
            if step == STEPS - 1:
                give(tile).start()
            return carry

        lax.fori_loop(0, slots, body, 0)

    def completed(value, ghost, below, above, j):
        pieces = []
        for zv in range(half // ROWS):
            piece = value[zv * ROWS : (zv + 1) * ROWS]
            piece = piece + jnp.where(at_edge[:ROWS], roll(ghost, -2 * (zv * columns + j)), zero)
            if zv == 0:
                piece = piece + jnp.where(first_row, below, zero)
            if zv == half // ROWS - 1:
                piece = piece + jnp.where(last_row, above, zero)
            pieces.append(piece)
        return jnp.concatenate(pieces, axis=0)

    def outer_step(step):
        later = (step + 1) % 2
        for tile in range(slots):
            for species in range(2):
                ghost = y_ghost[species, tile]
                for j in range(columns):
                    at = slice(j * LANES, (j + 1) * LANES)
                    field[later, species, tile, :, at] = completed(
                        field[later, species, tile, :, at], ghost,
                        z_ghost_low[species, tile : tile + 1, at],
                        z_ghost_high[species, tile : tile + 1, at], j)

    def give(tile):
        return pltpu.make_async_remote_copy(
            src_ref=field.at[STEPS % 2, other, tile], dst_ref=out.at[0, tile, own_rows, :],
            send_sem=out_send.at[tile], recv_sem=out_recv.at[tile],
            device_id=partner_id, device_id_type=MESH,
        )

    def take(tile):
        return pltpu.make_async_remote_copy(
            src_ref=field.at[STEPS % 2, other, tile], dst_ref=out.at[0, tile, other_rows, :],
            send_sem=out_send.at[tile], recv_sem=out_recv.at[tile],
            device_id=partner_id, device_id_type=MESH,
        )

    def last_copy(source, target, k, at, device):
        return pltpu.make_async_remote_copy(
            src_ref=source, dst_ref=target,
            send_sem=last_send.at[k], recv_sem=last_recv.at[at],
            device_id=device, device_id_type=MESH,
        )

    def last_sends():
        end = STEPS - 1
        both = jnp.logical_and
        result = []
        for s in range(2):
            target = core * 0 + s
            result += [
                (both(part == 0, has_down), last_copy(
                    z_low.at[end, s], z_last_plus, s, 0, {"cube": layer - 1, "pair": target})),
                (both(part == 1, has_up), last_copy(
                    z_high.at[end, s], z_last_minus, s, 1, {"cube": layer + 1, "pair": target})),
                (has_plus, last_copy(
                    y_last.at[s], y_last_minus.at[part], 2 + s, 2 + part,
                    {"row": band + 1, "pair": target})),
                (has_minus, last_copy(
                    y_last.at[s], y_last_plus.at[part], 4 + s, 4 + part,
                    {"row": band - 1, "pair": target})),
            ]
        return result + [
            (always, last_copy(y_last.at[other], y_last_here, 6, 6, partner_id)),
            (part == 0, last_copy(z_high.at[end, other], z_near, 7, 7, partner_id)),
            (part == 1, last_copy(z_low.at[end, other], z_near, 7, 7, partner_id)),
        ]

    def last_receives():
        arrivals = [(has_up, z_last_plus, 0), (has_down, z_last_minus, 1)]
        for h in range(2):
            arrivals.append((has_minus, y_last_minus.at[h], 2 + h))
            arrivals.append((has_plus, y_last_plus.at[h], 4 + h))
        arrivals += [(always, y_last_here, 6), (always, z_near, 7)]
        return [(wanted, last_copy(ref, ref, 0, at, partner_id)) for wanted, ref, at in arrivals]

    def last_step():
        rate = diffusion[core]
        first = part == 0
        end = STEPS - 1
        every = slice(None)
        for tile in range(slots):
            front_ok, front, front_here = entry(tile, 2)
            back_ok, back, back_here = entry(tile, 3)
            lower_ok, lower, _ = entry(tile, 4)
            upper_ok, upper, _ = entry(tile, 5)
            at = slice(tile, tile + 1)
            bottom = pick(lower_ok, z_last_minus, pl.ds(lower, 1), every)
            ceiling = pick(upper_ok, z_last_plus, pl.ds(upper, 1), every)
            near = z_near[at, :]
            mine = jnp.where(first, z_high[end, core, at, :], z_low[end, core, at, :])
            for h, rows in ((part, own_rows), (rest, other_rows)):
                if h is part:
                    front_in, back_in = y_last[core, front], y_last[core, back]
                    below = rate * jnp.where(first, bottom, near)
                    above = rate * jnp.where(first, near, ceiling)
                else:
                    front_in, back_in = y_last_here[front], y_last_here[back]
                    below = rate * jnp.where(first, mine, bottom)
                    above = rate * jnp.where(first, ceiling, mine)
                from_front = jnp.where(front_here, front_in, y_last_minus[h, front])
                from_back = jnp.where(back_here, back_in, y_last_plus[h, back])
                ghost = ghost_of(
                    rate, jnp.where(front_ok, from_front, zero), jnp.where(back_ok, from_back, zero), 0)
                for j in range(columns):
                    lanes = slice(j * LANES, (j + 1) * LANES)
                    if h is part:
                        value = field[STEPS % 2, core, tile, :, lanes]
                    else:
                        value = out[0, tile, rows, lanes]
                    out[0, tile, rows, lanes] = completed(
                        value, ghost, below[:, lanes], above[:, lanes], j)

    loads[0].wait()
    loads[1].wait()
    first_faces()
    pl.semaphore_wait(barrier, peers)
    for wanted, copy in first_sends():
        pl.when(wanted)(copy.start)
    swap.start()
    own_planes()
    for load in smalls:
        load.wait()
    loads[2].wait()
    swap_in.wait_recv()
    lax.fori_loop(0, slots, other_faces, 0, unroll=True)
    for step in range(STEPS - 1):
        inner_step(step)
        if step == 0:
            wait_first()
        else:
            wait_faces(step)
        compact(step)
        if step + 1 < STEPS - 1:
            send_faces(step + 1)
        else:
            for wanted, copy in last_sends():
                pl.when(wanted)(copy.start)
        outer_step(step)
    inner_step(STEPS - 1)
    for tile in range(slots):
        take(tile).wait_recv()
    for wanted, copy in last_receives():
        pl.when(wanted)(copy.wait_recv)
    last_step()
    swap.wait_send()
    for wanted, copy in first_sends():
        pl.when(wanted)(copy.wait_send)
    for step in range(1, STEPS - 1):
        wait_sent(step)
    for wanted, copy in last_sends():
        pl.when(wanted)(copy.wait_send)
    for tile in range(slots):
        give(tile).wait_send()


def per_device(layers, bands, ligand, density, counts, neighbours, diffusion, uptake):
    _, slots, depth, cells = ligand.shape
    half = depth // 2
    faces = (slots, ROWS, LANES)
    planes = (2, slots, cells)
    away = pl.BlockSpec(memory_space=pltpu.HBM)
    neighbours, diffusion, uptake = [
        pltpu.with_memory_space_constraint(x, pltpu.HBM) for x in (neighbours, diffusion, uptake)
    ]
    return pl.pallas_call(
        functools.partial(kernel, layers, bands, slots, half, cells),
        out_shape=jax.ShapeDtypeStruct(ligand.shape, jnp.float32),
        in_specs=[away] * 6,
        out_specs=pl.BlockSpec(memory_space=pltpu.VMEM),
        scratch_shapes=[
            pltpu.VMEM((2, 2, slots, half, cells), jnp.float32),
            pltpu.VMEM((slots, half, cells), jnp.int32),
            pltpu.VMEM((STEPS,) + faces, jnp.float32),
            pltpu.VMEM((STEPS,) + faces, jnp.float32),
            [pltpu.VMEM((2,) + faces, jnp.float32)] + [pltpu.VMEM(faces, jnp.float32)] * (STEPS - 2),
            [pltpu.VMEM((2,) + faces, jnp.float32)] + [pltpu.VMEM(faces, jnp.float32)] * (STEPS - 2),
            pltpu.VMEM((STEPS,) + planes, jnp.float32),
            pltpu.VMEM((STEPS,) + planes, jnp.float32),
            [pltpu.VMEM(planes, jnp.float32)] * (STEPS - 1),
            [pltpu.VMEM(planes, jnp.float32)] * (STEPS - 1),
            pltpu.VMEM((slots, half, cells), jnp.float32),
            pltpu.VMEM((2,) + faces, jnp.float32),
            pltpu.VMEM((2,) + faces, jnp.float32),
            pltpu.VMEM(planes, jnp.float32),
            pltpu.VMEM(planes, jnp.float32),
            pltpu.VMEM((2,) + faces, jnp.float32),
            pltpu.VMEM((2,) + faces, jnp.float32),
            pltpu.VMEM(planes, jnp.float32),
            pltpu.VMEM(planes, jnp.float32),
            pltpu.VMEM((2,) + faces, jnp.float32),
            pltpu.VMEM(faces, jnp.float32),
            pltpu.VMEM((2,) + faces, jnp.float32),
            pltpu.VMEM((2,) + faces, jnp.float32),
            pltpu.VMEM((slots, cells), jnp.float32),
            pltpu.VMEM((slots, cells), jnp.float32),
            pltpu.VMEM((slots, cells), jnp.float32),
            pltpu.SMEM((slots, 6), jnp.int32),
            pltpu.SMEM((1,), jnp.int32),
            pltpu.SMEM((2,), jnp.float32),
            pltpu.SMEM((2,), jnp.float32),
            pltpu.SemaphoreType.DMA((8,)),
            pltpu.SemaphoreType.DMA((4, 2)),
            pltpu.SemaphoreType.DMA((3,)),
            pltpu.SemaphoreType.DMA((4,)),
            pltpu.SemaphoreType.DMA,
            pltpu.SemaphoreType.DMA,
            pltpu.SemaphoreType.DMA((STEPS, 4)),
            pltpu.SemaphoreType.DMA((STEPS, 4)),
            pltpu.SemaphoreType.DMA((8,)),
            pltpu.SemaphoreType.DMA((8,)),
            pltpu.SemaphoreType.DMA((slots,)),
            pltpu.SemaphoreType.DMA((slots,)),
        ],
        compiler_params=pltpu.CompilerParams(
            collective_id=0, has_side_effects=True, vmem_limit_bytes=53 * 1024 * 1024
        ),
    )(neighbours, counts, diffusion, uptake, ligand, density)


def solution(mesh):
    in_specs = (
        P("pair", ("groups", "cube", "row"), None, None),
        P(("groups", "cube", "row"), None, None),
        P(("groups", "cube", "row")),
        P(("groups", "cube", "row"), None),
        P(),
        P(),
    )
    out_specs = P("pair", ("groups", "cube", "row"), None, None)
    return jax.shard_map(
        functools.partial(per_device, mesh.shape["cube"], mesh.shape["row"]),
        mesh=mesh, in_specs=in_specs, out_specs=out_specs, check_vma=False,
    )
```

```python
import functools

import jax
import jax.numpy as jnp
from jax import lax
from jax.experimental import pallas as pl
from jax.experimental.pallas import tpu as pltpu
from jax.sharding import PartitionSpec as P

EY = 32
STEPS = 4
DONE = {1: 1, 2: 4, 3: 3}
LANES = 128
ROWS = 8
MESH = pl.DeviceIdType.MESH


def kernel(
    layers, bands, slots, half, cells,
    nbr_in, counts_in, diffusion_in, uptake_in, ligand, density, out,
    field, dens, y_low, y_high, y_minus, y_plus, z_low, z_high, z_minus, z_plus,
    extra, y_first, y_here, z_first_low, z_first_high,
    y_part, y_ghost, z_ghost_low, z_ghost_high,
    y_last, y_last_here, y_last_minus, y_last_plus, z_last_minus, z_last_plus, z_near,
    line_high, line_low, solved_high, solved_low, near_front, near_back, far_front, far_back,
    g_front, g_back, g_below, g_above, weights,
    nbr, counts, diffusion, uptake,
    first_send, first_recv, load_sem, small_sem, swap_send, swap_recv, face_send, face_recv,
    line_send, line_recv, last_send, last_recv, out_send, out_recv,
):
    core = lax.axis_index("pair")
    layer = lax.axis_index("cube")
    band = lax.axis_index("row")
    block = layer * bands + band
    other = 1 - core
    part = lax.rem(core + band, 2)
    rest = 1 - part
    low_core = lax.rem(band, 2)
    high_core = 1 - low_core
    columns = cells // LANES
    has_minus = band > 0
    has_plus = band < bands - 1
    far_layer = jnp.where(part == 0, layer - 1, layer + 1)
    has_far = jnp.logical_and(far_layer >= 0, far_layer < layers)
    partner_id = {"pair": other}
    far_id = {"cube": far_layer, "pair": other}
    minus_id = {"row": band - 1, "pair": other}
    plus_id = {"row": band + 1, "pair": other}

    own_rows = pl.ds(pl.multiple_of(part * half, half), half)
    other_rows = pl.ds(pl.multiple_of(rest * half, half), half)
    loads = [
        pltpu.make_async_copy(ligand.at[0, :, own_rows, :], field.at[0, core], load_sem.at[0]),
        pltpu.make_async_copy(ligand.at[0, :, other_rows, :], extra, load_sem.at[2]),
        pltpu.make_async_copy(density.at[:, own_rows, :], dens, load_sem.at[1]),
    ]
    smalls = [
        pltpu.make_async_copy(source, target, small_sem.at[k])
        for k, (source, target) in enumerate(
            [(nbr_in, nbr), (counts_in, counts), (diffusion_in, diffusion), (uptake_in, uptake)]
        )
    ]
    for load in loads + smalls:
        load.start()

    barrier = pltpu.get_barrier_semaphore()
    has_down = layer > 0
    has_up = layer < layers - 1
    always = layer >= 0
    greeted = [
        (always, partner_id),
        (has_far, far_id),
        (has_down, {"cube": layer - 1}),
        (has_up, {"cube": layer + 1}),
        (has_minus, minus_id),
        (has_plus, plus_id),
        (has_minus, {"row": band - 1}),
        (has_plus, {"row": band + 1}),
        (jnp.logical_and(has_minus, has_far), {"row": band - 1, "cube": far_layer}),
        (jnp.logical_and(has_plus, has_far), {"row": band + 1, "cube": far_layer}),
    ]
    peers = jnp.int32(0)
    for wanted, device in greeted:
        pl.when(wanted)(
            functools.partial(
                pl.semaphore_signal, barrier, inc=1, device_id=device, device_id_type=MESH
            )
        )
        peers = peers + wanted.astype(jnp.int32)

    swap = pltpu.make_async_remote_copy(
        src_ref=ligand.at[0, :, other_rows, :], dst_ref=field.at[0, core],
        send_sem=swap_send, recv_sem=swap_recv, device_id=partner_id, device_id_type=MESH,
    )
    swap_in = pltpu.make_async_remote_copy(
        src_ref=ligand.at[0, :, other_rows, :], dst_ref=field.at[0, other],
        send_sem=swap_send, recv_sem=swap_recv, device_id=partner_id, device_id_type=MESH,
    )

    def remote(source, target, step, k, device):
        return pltpu.make_async_remote_copy(
            src_ref=source.at[step], dst_ref=target[step],
            send_sem=face_send.at[step, k], recv_sem=face_recv.at[step, k],
            device_id=device, device_id_type=MESH,
        )

    def messages(step):
        first, last = part == 0, part == 1
        up_far = remote(z_high, z_minus, step, 0, far_id)
        up_near = remote(z_high, z_minus, step, 0, partner_id)
        down_far = remote(z_low, z_plus, step, 1, far_id)
        down_near = remote(z_low, z_plus, step, 1, partner_id)
        to_plus = remote(y_high, y_minus, step, 2, plus_id)
        to_minus = remote(y_low, y_plus, step, 3, minus_id)
        both = jnp.logical_and
        sends = [
            (has_plus, to_plus), (has_minus, to_minus),
            (both(last, has_far), up_far), (both(first, has_far), down_far),
            (first, up_near), (last, down_near),
        ]
        receives = [
            (jnp.logical_or(last, has_far), up_near), (jnp.logical_or(first, has_far), down_near),
            (has_minus, to_plus), (has_plus, to_minus),
        ]
        return sends, receives

    def first_copy(source, target, k, at, device):
        return pltpu.make_async_remote_copy(
            src_ref=source, dst_ref=target.at[core],
            send_sem=first_send.at[k], recv_sem=first_recv.at[at, core],
            device_id=device, device_id_type=MESH,
        )

    def first_sends():
        return [
            (part == 0, first_copy(z_first_high.at[0], z_minus[0], 0, 0, partner_id)),
            (part == 1, first_copy(z_first_low.at[1], z_plus[0], 1, 1, partner_id)),
            (has_down, first_copy(
                z_first_low.at[0], z_plus[0], 2, 1, {"cube": layer - 1, "pair": high_core})),
            (has_up, first_copy(
                z_first_high.at[1], z_minus[0], 3, 0, {"cube": layer + 1, "pair": low_core})),
        ] + [
            (has_plus, first_copy(
                y_first.at[h], y_minus[0], 4 + h, 2, {"row": band + 1, "pair": lax.rem(band + 1 + h, 2)}))
            for h in range(2)
        ] + [
            (has_minus, first_copy(
                y_first.at[h], y_plus[0], 6 + h, 3, {"row": band - 1, "pair": lax.rem(band + 1 + h, 2)}))
            for h in range(2)
        ]

    def arrived(target, at, species):
        pltpu.make_async_remote_copy(
            src_ref=target.at[species], dst_ref=target.at[species],
            send_sem=first_send.at[0], recv_sem=first_recv.at[at, species],
            device_id=partner_id, device_id_type=MESH,
        ).wait_recv()

    def wait_first():
        both, either = jnp.logical_and, jnp.logical_or
        for species in range(2):
            across = core == 1 - species
            minus = either(both(part == 0, has_down), both(part == 1, across))
            plus = either(both(part == 1, has_up), both(part == 0, across))
            pl.when(minus)(functools.partial(arrived, z_minus[0], 0, species))
            pl.when(plus)(functools.partial(arrived, z_plus[0], 1, species))
            pl.when(has_minus)(functools.partial(arrived, y_minus[0], 2, species))
            pl.when(has_plus)(functools.partial(arrived, y_plus[0], 3, species))

    def send_faces(step):
        for wanted, copy in messages(step)[0]:
            pl.when(wanted)(copy.start)

    def wait_faces(step):
        for wanted, copy in messages(step)[1]:
            pl.when(wanted)(copy.wait_recv)

    def wait_sent(step):
        for wanted, copy in messages(step)[0]:
            pl.when(wanted)(copy.wait_send)

    lane = lax.broadcasted_iota(jnp.int32, (ROWS, LANES), 1)
    pair_of = lax.rem(lane + 1, EY) // 2
    even = lax.rem(lane, 2) == 0
    wide = lax.broadcasted_iota(jnp.int32, (half, LANES), 1)
    at_low = lax.rem(wide, EY) == 0
    at_high = lax.rem(wide, EY) == EY - 1
    at_edge = jnp.logical_or(at_low, at_high)
    below_32 = wide < EY
    above_96 = wide >= LANES - EY

    def roll(value, shift):
        shift = shift % LANES
        return value if shift == 0 else pltpu.roll(value, shift, axis=1)

    pieces = [(zv, j) for zv in range(half // ROWS) for j in range(columns)]

    def pack(parts):
        total = None
        for m, (zv, j) in enumerate(pieces):
            piece = roll(parts[j][zv * ROWS : (zv + 1) * ROWS], 2 * m)
            total = piece if total is None else jnp.where(pair_of == m, piece, total)
        return total

    def columns_of(value):
        return [value[:, j * LANES : (j + 1) * LANES] for j in range(columns)]

    def first_faces():
        for tile in range(slots):
            for h, value in ((part, field[0, core, tile]), (rest, extra[tile])):
                packed = pack(columns_of(value))
                y_first[h, tile] = packed
                z_first_low[h, tile : tile + 1, :] = value[:1]
                z_first_high[h, tile : tile + 1, :] = value[half - 1 :]
                if h is part:
                    y_here[core, tile] = packed

    def other_faces(tile, carry):
        y_here[other, tile] = pack(columns_of(field[0, other, tile]))
        return carry

    def own_planes():
        @pl.when(part == 0)
        def _():
            z_plus[0][core] = z_first_low[1]

        @pl.when(part == 1)
        def _():
            z_minus[0][core] = z_first_high[0]

    zero = jnp.float32(0.0)
    row = lax.broadcasted_iota(jnp.int32, (half, LANES), 0)

    def entry(tile, k):
        value = nbr[tile, k]
        safe = jnp.maximum(value, 0)
        return value >= 0, lax.rem(safe, slots), safe // slots == block

    def make_weights():
        source = lax.broadcasted_iota(jnp.int32, (2 * LANES, 2 * LANES), 0)
        target = lax.broadcasted_iota(jnp.int32, (2 * LANES, 2 * LANES), 1)
        apart = jnp.abs(source - target)
        same = source // EY == target // EY
        near = jnp.logical_or(apart == EY, jnp.logical_and(apart == 1, same))
        inside = jnp.where(near, 1.0, 0.0).astype(jnp.bfloat16)
        source = lax.broadcasted_iota(jnp.int32, (LANES, 2 * LANES), 0)
        target = lax.broadcasted_iota(jnp.int32, (LANES, 2 * LANES), 1)
        after = jnp.logical_and(source < EY, target == source + 2 * LANES - EY)
        before = jnp.logical_and(source >= LANES - EY, target == source - LANES + EY)
        beside = jnp.where(jnp.logical_or(after, before), 1.0, 0.0).astype(jnp.bfloat16)
        weights[: 2 * LANES, :] = inside
        weights[2 * LANES : 4 * LANES, :] = inside
        weights[4 * LANES : 5 * LANES, :] = beside
        weights[5 * LANES :, :] = beside

    def halves(value):
        high = value.astype(jnp.bfloat16)
        return high, (value - high.astype(jnp.float32)).astype(jnp.bfloat16)

    blocks = columns // 2

    def inner(step, tile, keep_faces):
        now, later = step % 2, (step + 1) % 2
        filled = tile < counts[0]
        left_ok, left, _ = entry(tile, 0)
        right_ok, right, _ = entry(tile, 1)
        fields, lefts = [], []
        for species in range(2):
            parts = columns_of(field[now, species, tile])
            if step == 0:
                parts = [jnp.where(filled, part, zero) for part in parts]
            fields.append(parts)
            ends = [
                jnp.where(left_ok, field[now, species, left, :, cells - LANES :], zero)
            ] + parts + [
                jnp.where(right_ok, field[now, species, right, :, :LANES], zero)
            ]
            split = [halves(part) for part in parts]
            for b in range(blocks):
                beside = halves(jnp.where(below_32, ends[2 * b + 3], ends[2 * b]))
                lefts.append(jnp.concatenate([
                    split[2 * b][0], split[2 * b + 1][0], split[2 * b][1], split[2 * b + 1][1],
                    beside[0], beside[1]], axis=1))
        sums = jnp.dot(
            jnp.concatenate(lefts, axis=0), weights[...], preferred_element_type=jnp.float32)
        amount = columns_of(dens[tile])
        share = [
            amount[j].astype(jnp.float32) / (1.0 + fields[0][j] + fields[1][j])
            for j in range(columns)
        ]
        blank = jnp.zeros((1, LANES), jnp.float32)
        for species in range(2):
            parts = fields[species]
            rate = diffusion[species]
            keep = 1.0 - 6.0 * rate
            taken = uptake[species] * 0.125
            values = []
            for j in range(columns):
                part = parts[j]
                at = (species * blocks + j // 2) * half
                value = sums[at : at + half, (j % 2) * LANES : (j % 2 + 1) * LANES]
                value = value + jnp.concatenate([blank, part[: half - 1]], axis=0)
                value = value + jnp.concatenate([part[1:], blank], axis=0)
                value = part * (keep - taken * share[j]) + rate * value
                field[later, species, tile, :, j * LANES : (j + 1) * LANES] = value
                values.append(value)
            if keep_faces:
                y_part[species, tile] = pack(values)

    top = (half // ROWS - 1) * columns
    sub = lax.broadcasted_iota(jnp.int32, (ROWS, LANES), 0)
    in_low = jnp.logical_and(sub == 0, pair_of < columns)
    in_high = jnp.logical_and(sub == ROWS - 1, pair_of >= top)
    first_row = sub == 0
    last_row = sub == ROWS - 1
    row_pair = lax.rem(lax.broadcasted_iota(jnp.int32, (slots, LANES), 1) + 1, EY) // 2
    row_edge = row_pair == 0

    def pick(ok, ref, *at):
        return jnp.where(ok, ref[at], zero)

    def ghost_of(rate, from_front, from_back, shift):
        return rate * jnp.where(
            even, roll(from_front, 1 - EY - shift), roll(from_back, EY - 1 - shift)
        )

    def compact(step):
        into = DONE[step + 1]
        later = (step + 1) % 2
        first = part == 0
        for tile in range(slots):
            filled = tile < counts[0]
            front_ok, front, front_here = entry(tile, 2)
            back_ok, back, back_here = entry(tile, 3)
            lower_ok, lower, _ = entry(tile, 4)
            upper_ok, upper, _ = entry(tile, 5)
            lower = jnp.where(first, lower, tile)
            lower_ok = jnp.where(first, lower_ok, filled)
            upper = jnp.where(first, tile, upper)
            upper_ok = jnp.where(first, filled, upper_ok)
            for species in range(2):
                rate = diffusion[species]
                if step == 0:
                    shift = 0
                    from_front = jnp.where(
                        front_here, y_here[species, front], y_minus[0][species, front])
                    from_back = jnp.where(
                        back_here, y_here[species, back], y_plus[0][species, back])
                elif step == 1:
                    shift = species
                    from_front = jnp.where(front_here, y_high[step, front], y_minus[step][front])
                    from_back = jnp.where(back_here, y_low[step, back], y_plus[step][back])
                else:
                    shift = species
                    from_front = jnp.where(front_here, y_high[DONE[step], front], g_front[tile])
                    from_back = jnp.where(back_here, y_low[DONE[step], back], g_back[tile])
                from_front = jnp.where(front_ok, from_front, zero)
                from_back = jnp.where(back_ok, from_back, zero)
                y_ghost[species, tile] = ghost_of(rate, from_front, from_back, shift)
                at = slice(tile, tile + 1)
                if step < 2:
                    below = pick(lower_ok, z_minus[step], species, pl.ds(lower, 1), slice(None))
                    above = pick(upper_ok, z_plus[step], species, pl.ds(upper, 1), slice(None))
                else:
                    below = pick(lower_ok, g_below, species, at, slice(None))
                    above = pick(upper_ok, g_above, species, at, slice(None))
                below = rate * below
                above = rate * above
                z_ghost_low[species, at, :] = below
                z_ghost_high[species, at, :] = above
                z_low[into, species, at, :] = field[later, species, tile, :1, :] + below
                z_high[into, species, at, :] = field[later, species, tile, half - 1 :, :] + above
        packed = []
        for species in range(2):
            ghosts = [y_ghost[species, tile] for tile in range(slots)]
            edge_low = jnp.concatenate([ghost[:1] for ghost in ghosts], axis=0)
            edge_high = jnp.concatenate([ghost[ROWS - 1 :] for ghost in ghosts], axis=0)
            pack_low = jnp.zeros((slots, LANES), jnp.float32)
            pack_high = jnp.zeros((slots, LANES), jnp.float32)
            for j in range(columns):
                at = slice(j * LANES, (j + 1) * LANES)
                low = roll(z_ghost_low[species, :, at], 2 * j)
                high = roll(z_ghost_high[species, :, at], 2 * (top + j))
                pack_low = jnp.where(row_pair == j, low, pack_low)
                pack_high = jnp.where(row_pair == top + j, high, pack_high)
                z_low[into, species, :, at] += jnp.where(row_edge, roll(edge_low, -2 * j), zero)
                z_high[into, species, :, at] += jnp.where(
                    row_edge, roll(edge_high, -2 * (top + j)), zero)
            packed.append([
                y_part[species, tile] + ghosts[tile]
                + jnp.where(in_low, jnp.broadcast_to(pack_low[tile : tile + 1], (ROWS, LANES)), zero)
                + jnp.where(in_high, jnp.broadcast_to(pack_high[tile : tile + 1], (ROWS, LANES)), zero)
                for tile in range(slots)
            ])
        for tile in range(slots):
            if step + 1 == STEPS - 1:
                for species in range(2):
                    y_last[species, tile] = packed[species][tile]
            else:
                second = roll(packed[1][tile], 1)
                y_low[into, tile] = jnp.where(even, packed[0][tile], second)
                y_high[into, tile] = jnp.where(even, second, packed[0][tile])

    lines = lax.broadcasted_iota(jnp.int32, (slots, LANES), 1)
    line_even = lax.rem(lines, 2) == 0
    in_low_format = lax.rem(lane, EY) // 2

    def rows_of(rows):
        return jnp.concatenate(rows, axis=0)

    def line_ghost(rate, from_front, from_back, shift):
        return rate * jnp.where(
            line_even, roll(from_front, 1 - EY - shift), roll(from_back, EY - 1 - shift)
        )

    def line_copy(source, target, k, device):
        return pltpu.make_async_remote_copy(
            src_ref=source, dst_ref=target, send_sem=line_send.at[k], recv_sem=line_recv.at[k],
            device_id=device, device_id_type=MESH,
        )

    def line_messages():
        both = jnp.logical_and
        out_and_in = [
            (has_plus, has_minus, line_high, near_front, {"row": band + 1}),
            (has_minus, has_plus, line_low, near_back, {"row": band - 1}),
            (both(has_plus, has_far), both(has_minus, has_far), solved_high, far_front,
             {"row": band + 1, "cube": far_layer}),
            (both(has_minus, has_far), both(has_plus, has_far), solved_low, far_back,
             {"row": band - 1, "cube": far_layer}),
        ]
        return [
            (sent, received, line_copy(source, target, k, device))
            for k, (sent, received, source, target, device) in enumerate(out_and_in)
        ]

    def make_lines():
        for tile in range(slots):
            at = slice(tile, tile + 1)
            high, low = y_high[1, tile], y_low[1, tile]
            line_high[at, :] = jnp.where(pair_of[:1] < columns, high[:1], high[ROWS - 1 :])
            line_low[at, :] = jnp.where(in_low_format[:1] < columns, low[:1], low[ROWS - 1 :])
        for k, column in ((0, None), (1, 3)):
            solve(line_high, solved_high, k, column)
        for k, column in ((0, None), (1, 2)):
            solve(line_low, solved_low, k, column)

    def solve(line, solved, k, column):
        names = []
        for tile in range(slots):
            if column is None:
                value = jnp.where(part == 0, nbr[tile, 4], nbr[tile, 5])
                names.append(jnp.where(value >= 0, lax.rem(jnp.maximum(value, 0), slots), -1))
            else:
                ok, slot, here = entry(tile, column)
                names.append(jnp.where(jnp.logical_and(ok, jnp.logical_not(here)), slot, -1))
        found = lax.broadcasted_iota(jnp.int32, (slots, LANES), 0)
        total = jnp.zeros((slots, LANES), jnp.float32)
        for tile in range(slots):
            row = jnp.broadcast_to(line[tile : tile + 1, :], (slots, LANES))
            total = total + jnp.where(found == names[tile], row, zero)
        solved[k] = total

    def partial_faces(step):
        later = (step + 1) % 2
        into = step + 1
        fronts, backs = [], []
        for tile in range(slots):
            second = roll(y_part[1, tile], 1)
            y_low[into, tile] = jnp.where(even, y_part[0, tile], second)
            y_high[into, tile] = jnp.where(even, second, y_part[0, tile])
            front_ok, front, front_here = entry(tile, 2)
            back_ok, back, back_here = entry(tile, 3)
            both = jnp.logical_and
            fronts.append(pick(both(front_ok, front_here), line_high, pl.ds(front, 1), slice(None)))
            backs.append(pick(both(back_ok, back_here), line_low, pl.ds(back, 1), slice(None)))
            for species in range(2):
                at = slice(tile, tile + 1)
                z_low[into, species, at, :] = field[later, species, tile, :1, :]
                z_high[into, species, at, :] = field[later, species, tile, half - 1 :, :]
        fronts, backs = rows_of(fronts), rows_of(backs)
        for species in range(2):
            edge = line_ghost(diffusion[species], fronts, backs, species)
            for j in range(columns):
                at = slice(j * LANES, (j + 1) * LANES)
                z_low[into, species, :, at] += jnp.where(row_edge, roll(edge, -2 * j), zero)
                z_high[into, species, :, at] += jnp.where(
                    row_edge, roll(edge, -2 * (top + j)), zero)

    def complete(step):
        first = part == 0
        both = jnp.logical_and
        every = slice(None)
        shift = 2 * top
        low_even_rate = jnp.where(even, diffusion[0], diffusion[1])
        high_even_rate = jnp.where(even, diffusion[1], diffusion[0])
        below_front, below_back, above_front, above_back = [], [], [], []
        for tile in range(slots):
            front_ok, front, front_here = entry(tile, 2)
            back_ok, back, back_here = entry(tile, 3)
            lower_ok, lower, _ = entry(tile, 4)
            upper_ok, upper, _ = entry(tile, 5)
            far = jnp.where(first, lower, upper)
            far_ok = jnp.where(first, lower_ok, upper_ok)
            front_cross = both(front_ok, jnp.logical_not(front_here))
            back_cross = both(back_ok, jnp.logical_not(back_here))
            near_f = pick(front_cross, near_front, pl.ds(front, 1), every)
            near_b = pick(back_cross, near_back, pl.ds(back, 1), every)
            side_f = pick(both(front_cross, has_far), far_front, 0, pl.ds(front, 1), every)
            side_b = pick(both(back_cross, has_far), far_back, 0, pl.ds(back, 1), every)
            far_f = pick(both(far_ok, has_minus), far_front, 1, pl.ds(far, 1), every)
            far_b = pick(both(far_ok, has_plus), far_back, 1, pl.ds(far, 1), every)
            below_front.append(jnp.where(first, far_f, near_f))
            above_front.append(jnp.where(first, near_f, far_f))
            below_back.append(jnp.where(first, far_b, near_b))
            above_back.append(jnp.where(first, near_b, far_b))

            def placed(near, side, form):
                low = roll(jnp.broadcast_to(jnp.where(first, side, near), (ROWS, LANES)), -shift)
                high = roll(jnp.broadcast_to(jnp.where(first, near, side), (ROWS, LANES)), shift)
                low = jnp.where(both(sub == 0, form < columns), low, zero)
                return low + jnp.where(both(sub == ROWS - 1, form >= top), high, zero)

            g_front[tile] = jnp.where(
                front_cross,
                y_minus[step + 1][front] + high_even_rate * (
                    roll(y_low[step, tile], EY - 1) + placed(near_f, side_f, pair_of)),
                zero)
            g_back[tile] = jnp.where(
                back_cross,
                y_plus[step + 1][back] + low_even_rate * (
                    roll(y_high[step, tile], 1 - EY) + placed(near_b, side_b, in_low_format)),
                zero)
            lower = jnp.where(first, lower, tile)
            upper = jnp.where(first, tile, upper)
            for species in range(2):
                rate = diffusion[species]
                at = slice(tile, tile + 1)
                g_below[species, at, :] = (
                    z_minus[step + 1][species, pl.ds(lower, 1), :] + rate * z_low[step, species, at, :])
                g_above[species, at, :] = (
                    z_plus[step + 1][species, pl.ds(upper, 1), :] + rate * z_high[step, species, at, :])
        below_front, below_back = rows_of(below_front), rows_of(below_back)
        above_front, above_back = rows_of(above_front), rows_of(above_back)
        for species in range(2):
            below = line_ghost(diffusion[species], below_front, below_back, species)
            above = line_ghost(diffusion[species], above_front, above_back, species)
            for j in range(columns):
                at = slice(j * LANES, (j + 1) * LANES)
                g_below[species, :, at] += jnp.where(
                    row_edge, roll(below, -2 * (top + j)), zero)
                g_above[species, :, at] += jnp.where(row_edge, roll(above, -2 * j), zero)

    def inner_step(step):
        for tile in range(slots):
            inner(step, tile, step < STEPS - 1)
            if step == STEPS - 1:
                give(tile).start()

    def completed(value, ghost, below, above, j):
        pieces = []
        for zv in range(half // ROWS):
            piece = value[zv * ROWS : (zv + 1) * ROWS]
            piece = piece + jnp.where(at_edge[:ROWS], roll(ghost, -2 * (zv * columns + j)), zero)
            if zv == 0:
                piece = piece + jnp.where(first_row, below, zero)
            if zv == half // ROWS - 1:
                piece = piece + jnp.where(last_row, above, zero)
            pieces.append(piece)
        return jnp.concatenate(pieces, axis=0)

    def outer_step(step):
        later = (step + 1) % 2
        for tile in range(slots):
            for species in range(2):
                ghost = y_ghost[species, tile]
                for j in range(columns):
                    at = slice(j * LANES, (j + 1) * LANES)
                    field[later, species, tile, :, at] = completed(
                        field[later, species, tile, :, at], ghost,
                        z_ghost_low[species, tile : tile + 1, at],
                        z_ghost_high[species, tile : tile + 1, at], j)

    def give(tile):
        return pltpu.make_async_remote_copy(
            src_ref=field.at[STEPS % 2, other, tile], dst_ref=out.at[0, tile, own_rows, :],
            send_sem=out_send.at[tile], recv_sem=out_recv.at[tile],
            device_id=partner_id, device_id_type=MESH,
        )

    def take(tile):
        return pltpu.make_async_remote_copy(
            src_ref=field.at[STEPS % 2, other, tile], dst_ref=out.at[0, tile, other_rows, :],
            send_sem=out_send.at[tile], recv_sem=out_recv.at[tile],
            device_id=partner_id, device_id_type=MESH,
        )

    def last_copy(source, target, k, at, device):
        return pltpu.make_async_remote_copy(
            src_ref=source, dst_ref=target,
            send_sem=last_send.at[k], recv_sem=last_recv.at[at],
            device_id=device, device_id_type=MESH,
        )

    def last_sends():
        end = STEPS - 1
        both = jnp.logical_and
        result = []
        for s in range(2):
            target = core * 0 + s
            result += [
                (both(part == 0, has_down), last_copy(
                    z_low.at[end, s], z_last_plus, s, 0, {"cube": layer - 1, "pair": target})),
                (both(part == 1, has_up), last_copy(
                    z_high.at[end, s], z_last_minus, s, 1, {"cube": layer + 1, "pair": target})),
                (has_plus, last_copy(
                    y_last.at[s], y_last_minus.at[part], 2 + s, 2 + part,
                    {"row": band + 1, "pair": target})),
                (has_minus, last_copy(
                    y_last.at[s], y_last_plus.at[part], 4 + s, 4 + part,
                    {"row": band - 1, "pair": target})),
            ]
        return result + [
            (always, last_copy(y_last.at[other], y_last_here, 6, 6, partner_id)),
            (part == 0, last_copy(z_high.at[end, other], z_near, 7, 7, partner_id)),
            (part == 1, last_copy(z_low.at[end, other], z_near, 7, 7, partner_id)),
        ]

    def last_receives():
        arrivals = [(has_up, z_last_plus, 0), (has_down, z_last_minus, 1)]
        for h in range(2):
            arrivals.append((has_minus, y_last_minus.at[h], 2 + h))
            arrivals.append((has_plus, y_last_plus.at[h], 4 + h))
        arrivals += [(always, y_last_here, 6), (always, z_near, 7)]
        return [(wanted, last_copy(ref, ref, 0, at, partner_id)) for wanted, ref, at in arrivals]

    def last_step():
        rate = diffusion[core]
        first = part == 0
        end = STEPS - 1
        every = slice(None)
        for tile in range(slots):
            front_ok, front, front_here = entry(tile, 2)
            back_ok, back, back_here = entry(tile, 3)
            lower_ok, lower, _ = entry(tile, 4)
            upper_ok, upper, _ = entry(tile, 5)
            at = slice(tile, tile + 1)
            bottom = pick(lower_ok, z_last_minus, pl.ds(lower, 1), every)
            ceiling = pick(upper_ok, z_last_plus, pl.ds(upper, 1), every)
            near = z_near[at, :]
            mine = jnp.where(first, z_high[end, core, at, :], z_low[end, core, at, :])
            for h, rows in ((part, own_rows), (rest, other_rows)):
                if h is part:
                    front_in, back_in = y_last[core, front], y_last[core, back]
                    below = rate * jnp.where(first, bottom, near)
                    above = rate * jnp.where(first, near, ceiling)
                else:
                    front_in, back_in = y_last_here[front], y_last_here[back]
                    below = rate * jnp.where(first, mine, bottom)
                    above = rate * jnp.where(first, ceiling, mine)
                from_front = jnp.where(front_here, front_in, y_last_minus[h, front])
                from_back = jnp.where(back_here, back_in, y_last_plus[h, back])
                ghost = ghost_of(
                    rate, jnp.where(front_ok, from_front, zero), jnp.where(back_ok, from_back, zero), 0)
                for j in range(columns):
                    lanes = slice(j * LANES, (j + 1) * LANES)
                    if h is part:
                        value = field[STEPS % 2, core, tile, :, lanes]
                    else:
                        value = out[0, tile, rows, lanes]
                    out[0, tile, rows, lanes] = completed(
                        value, ghost, below[:, lanes], above[:, lanes], j)

    loads[0].wait()
    loads[1].wait()
    make_weights()
    first_faces()
    pl.semaphore_wait(barrier, peers)
    for wanted, copy in first_sends():
        pl.when(wanted)(copy.start)
    swap.start()
    own_planes()
    for load in smalls:
        load.wait()
    loads[2].wait()
    swap_in.wait_recv()
    lax.fori_loop(0, slots, other_faces, 0, unroll=True)
    inner_step(0)
    wait_first()
    compact(0)
    send_faces(1)
    make_lines()
    for sent, _, copy in line_messages():
        pl.when(sent)(copy.start)
    outer_step(0)
    inner_step(1)
    partial_faces(1)
    send_faces(2)
    wait_faces(1)
    compact(1)
    outer_step(1)
    inner_step(2)
    wait_faces(2)
    for _, received, copy in line_messages():
        pl.when(received)(copy.wait_recv)
    complete(1)
    compact(2)
    for wanted, copy in last_sends():
        pl.when(wanted)(copy.start)
    outer_step(2)
    inner_step(STEPS - 1)
    for tile in range(slots):
        take(tile).wait_recv()
    for wanted, copy in last_receives():
        pl.when(wanted)(copy.wait_recv)
    last_step()
    swap.wait_send()
    for wanted, copy in first_sends():
        pl.when(wanted)(copy.wait_send)
    for step in range(1, STEPS - 1):
        wait_sent(step)
    for sent, _, copy in line_messages():
        pl.when(sent)(copy.wait_send)
    for wanted, copy in last_sends():
        pl.when(wanted)(copy.wait_send)
    for tile in range(slots):
        give(tile).wait_send()


def per_device(layers, bands, ligand, density, counts, neighbours, diffusion, uptake):
    _, slots, depth, cells = ligand.shape
    half = depth // 2
    faces = (slots, ROWS, LANES)
    planes = (2, slots, cells)
    away = pl.BlockSpec(memory_space=pltpu.HBM)
    neighbours, diffusion, uptake = [
        pltpu.with_memory_space_constraint(x, pltpu.HBM) for x in (neighbours, diffusion, uptake)
    ]
    return pl.pallas_call(
        functools.partial(kernel, layers, bands, slots, half, cells),
        out_shape=jax.ShapeDtypeStruct(ligand.shape, jnp.float32),
        in_specs=[away] * 6,
        out_specs=pl.BlockSpec(memory_space=pltpu.VMEM),
        scratch_shapes=[
            pltpu.VMEM((2, 2, slots, half, cells), jnp.float32),
            pltpu.VMEM((slots, half, cells), jnp.int32),
            pltpu.VMEM((STEPS + 1,) + faces, jnp.float32),
            pltpu.VMEM((STEPS + 1,) + faces, jnp.float32),
            [pltpu.VMEM((2,) + faces, jnp.float32)] + [pltpu.VMEM(faces, jnp.float32)] * (STEPS - 2),
            [pltpu.VMEM((2,) + faces, jnp.float32)] + [pltpu.VMEM(faces, jnp.float32)] * (STEPS - 2),
            pltpu.VMEM((STEPS + 1,) + planes, jnp.float32),
            pltpu.VMEM((STEPS + 1,) + planes, jnp.float32),
            [pltpu.VMEM(planes, jnp.float32)] * (STEPS - 1),
            [pltpu.VMEM(planes, jnp.float32)] * (STEPS - 1),
            pltpu.VMEM((slots, half, cells), jnp.float32),
            pltpu.VMEM((2,) + faces, jnp.float32),
            pltpu.VMEM((2,) + faces, jnp.float32),
            pltpu.VMEM(planes, jnp.float32),
            pltpu.VMEM(planes, jnp.float32),
            pltpu.VMEM((2,) + faces, jnp.float32),
            pltpu.VMEM((2,) + faces, jnp.float32),
            pltpu.VMEM(planes, jnp.float32),
            pltpu.VMEM(planes, jnp.float32),
            pltpu.VMEM((2,) + faces, jnp.float32),
            pltpu.VMEM(faces, jnp.float32),
            pltpu.VMEM((2,) + faces, jnp.float32),
            pltpu.VMEM((2,) + faces, jnp.float32),
            pltpu.VMEM((slots, cells), jnp.float32),
            pltpu.VMEM((slots, cells), jnp.float32),
            pltpu.VMEM((slots, cells), jnp.float32),
            pltpu.VMEM((slots, LANES), jnp.float32),
            pltpu.VMEM((slots, LANES), jnp.float32),
            pltpu.VMEM((2, slots, LANES), jnp.float32),
            pltpu.VMEM((2, slots, LANES), jnp.float32),
            pltpu.VMEM((slots, LANES), jnp.float32),
            pltpu.VMEM((slots, LANES), jnp.float32),
            pltpu.VMEM((2, slots, LANES), jnp.float32),
            pltpu.VMEM((2, slots, LANES), jnp.float32),
            pltpu.VMEM(faces, jnp.float32),
            pltpu.VMEM(faces, jnp.float32),
            pltpu.VMEM(planes, jnp.float32),
            pltpu.VMEM(planes, jnp.float32),
            pltpu.VMEM((6 * LANES, 2 * LANES), jnp.bfloat16),
            pltpu.SMEM((slots, 6), jnp.int32),
            pltpu.SMEM((1,), jnp.int32),
            pltpu.SMEM((2,), jnp.float32),
            pltpu.SMEM((2,), jnp.float32),
            pltpu.SemaphoreType.DMA((8,)),
            pltpu.SemaphoreType.DMA((4, 2)),
            pltpu.SemaphoreType.DMA((3,)),
            pltpu.SemaphoreType.DMA((4,)),
            pltpu.SemaphoreType.DMA,
            pltpu.SemaphoreType.DMA,
            pltpu.SemaphoreType.DMA((STEPS, 4)),
            pltpu.SemaphoreType.DMA((STEPS, 4)),
            pltpu.SemaphoreType.DMA((4,)),
            pltpu.SemaphoreType.DMA((4,)),
            pltpu.SemaphoreType.DMA((8,)),
            pltpu.SemaphoreType.DMA((8,)),
            pltpu.SemaphoreType.DMA((slots,)),
            pltpu.SemaphoreType.DMA((slots,)),
        ],
        compiler_params=pltpu.CompilerParams(
            collective_id=0, has_side_effects=True, vmem_limit_bytes=53 * 1024 * 1024
        ),
    )(neighbours, counts, diffusion, uptake, ligand, density)


def solution(mesh):
    in_specs = (
        P("pair", ("groups", "cube", "row"), None, None),
        P(("groups", "cube", "row"), None, None),
        P(("groups", "cube", "row")),
        P(("groups", "cube", "row"), None),
        P(),
        P(),
    )
    out_specs = P("pair", ("groups", "cube", "row"), None, None)
    return jax.shard_map(
        functools.partial(per_device, mesh.shape["cube"], mesh.shape["row"]),
        mesh=mesh, in_specs=in_specs, out_specs=out_specs, check_vma=False,
    )
```

```python
import functools

import jax
import jax.numpy as jnp
from jax import lax
from jax.experimental import pallas as pl
from jax.experimental.pallas import tpu as pltpu
from jax.sharding import PartitionSpec as P

EY = 32
STEPS = 4
DONE = {1: 1, 2: 4, 3: 3}
LANES = 128
ROWS = 8
MESH = pl.DeviceIdType.MESH


def kernel(
    layers, bands, slots, half, cells,
    nbr_in, counts_in, diffusion_in, uptake_in, ligand, density, out,
    field, dens, y_low, y_high, y_minus, y_plus, z_low, z_high, z_minus, z_plus,
    extra, y_first_low, y_first_high, y_here, z_first_low, z_first_high,
    y_part, y_ghost, z_ghost_low, z_ghost_high,
    y_last, y_last_low, y_last_high, y_last_here, y_last_minus, y_last_plus, z_last_minus, z_last_plus, z_near,
    line_high, line_low, solved_high, solved_low, near_front, near_back, far_front, far_back,
    g_front, g_back, g_below, g_above, weights,
    nbr, counts, diffusion, uptake,
    first_send, first_recv, load_sem, small_sem, swap_send, swap_recv, face_send, face_recv,
    line_send, line_recv, last_send, last_recv, out_send, out_recv,
):
    core = lax.axis_index("pair")
    layer = lax.axis_index("cube")
    band = lax.axis_index("row")
    block = layer * bands + band
    other = 1 - core
    part = lax.rem(core + band, 2)
    rest = 1 - part
    low_core = lax.rem(band, 2)
    high_core = 1 - low_core
    columns = cells // LANES
    has_minus = band > 0
    has_plus = band < bands - 1
    far_layer = jnp.where(part == 0, layer - 1, layer + 1)
    has_far = jnp.logical_and(far_layer >= 0, far_layer < layers)
    partner_id = {"pair": other}
    far_id = {"cube": far_layer, "pair": other}
    minus_id = {"row": band - 1, "pair": other}
    plus_id = {"row": band + 1, "pair": other}

    own_rows = pl.ds(pl.multiple_of(part * half, half), half)
    other_rows = pl.ds(pl.multiple_of(rest * half, half), half)
    loads = [
        pltpu.make_async_copy(ligand.at[0, :, own_rows, :], field.at[0, core], load_sem.at[0]),
        pltpu.make_async_copy(ligand.at[0, :, other_rows, :], extra, load_sem.at[2]),
        pltpu.make_async_copy(density.at[:, own_rows, :], dens, load_sem.at[1]),
    ]
    smalls = [
        pltpu.make_async_copy(source, target, small_sem.at[k])
        for k, (source, target) in enumerate(
            [(nbr_in, nbr), (counts_in, counts), (diffusion_in, diffusion), (uptake_in, uptake)]
        )
    ]

    barrier = pltpu.get_barrier_semaphore()
    has_down = layer > 0
    has_up = layer < layers - 1
    always = layer >= 0
    greeted = [
        (always, partner_id),
        (has_far, far_id),
        (has_down, {"cube": layer - 1}),
        (has_up, {"cube": layer + 1}),
        (has_minus, minus_id),
        (has_plus, plus_id),
        (has_minus, {"row": band - 1}),
        (has_plus, {"row": band + 1}),
        (jnp.logical_and(has_minus, has_far), {"row": band - 1, "cube": far_layer}),
        (jnp.logical_and(has_plus, has_far), {"row": band + 1, "cube": far_layer}),
    ]
    peers = jnp.int32(0)
    for wanted, device in greeted:
        pl.when(wanted)(
            functools.partial(
                pl.semaphore_signal, barrier, inc=1, device_id=device, device_id_type=MESH
            )
        )
        peers = peers + wanted.astype(jnp.int32)

    for load in loads + smalls:
        load.start()

    swap = pltpu.make_async_remote_copy(
        src_ref=ligand.at[0, :, other_rows, :], dst_ref=field.at[0, core],
        send_sem=swap_send, recv_sem=swap_recv, device_id=partner_id, device_id_type=MESH,
    )
    swap_in = pltpu.make_async_remote_copy(
        src_ref=ligand.at[0, :, other_rows, :], dst_ref=field.at[0, other],
        send_sem=swap_send, recv_sem=swap_recv, device_id=partner_id, device_id_type=MESH,
    )

    def remote(source, target, step, k, device):
        return pltpu.make_async_remote_copy(
            src_ref=source.at[step], dst_ref=target[step],
            send_sem=face_send.at[step, k], recv_sem=face_recv.at[step, k],
            device_id=device, device_id_type=MESH,
        )

    def messages(step):
        first, last = part == 0, part == 1
        up_far = remote(z_high, z_minus, step, 0, far_id)
        up_near = remote(z_high, z_minus, step, 0, partner_id)
        down_far = remote(z_low, z_plus, step, 1, far_id)
        down_near = remote(z_low, z_plus, step, 1, partner_id)
        to_plus = remote(y_high, y_minus, step, 2, plus_id)
        to_minus = remote(y_low, y_plus, step, 3, minus_id)
        both = jnp.logical_and
        sends = [
            (has_plus, to_plus), (has_minus, to_minus),
            (both(last, has_far), up_far), (both(first, has_far), down_far),
            (first, up_near), (last, down_near),
        ]
        receives = [
            (jnp.logical_or(last, has_far), up_near), (jnp.logical_or(first, has_far), down_near),
            (has_minus, to_plus), (has_plus, to_minus),
        ]
        return sends, receives

    def first_copy(source, target, k, at, device):
        return pltpu.make_async_remote_copy(
            src_ref=source, dst_ref=target.at[core],
            send_sem=first_send.at[k], recv_sem=first_recv.at[at, core],
            device_id=device, device_id_type=MESH,
        )

    def first_sends():
        return [
            (has_plus, first_copy(
                y_first_high.at[h], y_minus[0], 4 + h, 2, {"row": band + 1, "pair": lax.rem(band + 1 + h, 2)}))
            for h in range(2)
        ] + [
            (has_minus, first_copy(
                y_first_low.at[h], y_plus[0], 6 + h, 3, {"row": band - 1, "pair": lax.rem(band + 1 + h, 2)}))
            for h in range(2)
        ] + [
            (has_down, first_copy(
                z_first_low.at[0], z_plus[0], 2, 1, {"cube": layer - 1, "pair": high_core})),
            (has_up, first_copy(
                z_first_high.at[1], z_minus[0], 3, 0, {"cube": layer + 1, "pair": low_core})),
            (part == 0, first_copy(z_first_high.at[0], z_minus[0], 0, 0, partner_id)),
            (part == 1, first_copy(z_first_low.at[1], z_plus[0], 1, 1, partner_id)),
        ]

    def arrived(target, at, species):
        pltpu.make_async_remote_copy(
            src_ref=target.at[species], dst_ref=target.at[species],
            send_sem=first_send.at[0], recv_sem=first_recv.at[at, species],
            device_id=partner_id, device_id_type=MESH,
        ).wait_recv()

    def wait_first():
        both, either = jnp.logical_and, jnp.logical_or
        for species in range(2):
            across = core == 1 - species
            minus = either(both(part == 0, has_down), both(part == 1, across))
            plus = either(both(part == 1, has_up), both(part == 0, across))
            pl.when(minus)(functools.partial(arrived, z_minus[0], 0, species))
            pl.when(plus)(functools.partial(arrived, z_plus[0], 1, species))
            pl.when(has_minus)(functools.partial(arrived, y_minus[0], 2, species))
            pl.when(has_plus)(functools.partial(arrived, y_plus[0], 3, species))

    def send_faces(step):
        for wanted, copy in messages(step)[0]:
            pl.when(wanted)(copy.start)

    def wait_faces(step):
        for wanted, copy in messages(step)[1]:
            pl.when(wanted)(copy.wait_recv)

    def wait_sent(step):
        for wanted, copy in messages(step)[0]:
            pl.when(wanted)(copy.wait_send)

    lane = lax.broadcasted_iota(jnp.int32, (ROWS, LANES), 1)
    pair_of = lax.rem(lane + 1, EY) // 2
    even = lax.rem(lane, 2) == 0
    wide = lax.broadcasted_iota(jnp.int32, (half, LANES), 1)
    at_low = lax.rem(wide, EY) == 0
    at_high = lax.rem(wide, EY) == EY - 1
    at_edge = jnp.logical_or(at_low, at_high)
    below_32 = wide < EY
    above_96 = wide >= LANES - EY

    def roll(value, shift):
        shift = shift % LANES
        return value if shift == 0 else pltpu.roll(value, shift, axis=1)

    pieces = [(zv, j) for zv in range(half // ROWS) for j in range(columns)]

    def pack(parts):
        total = None
        for m, (zv, j) in enumerate(pieces):
            piece = roll(parts[j][zv * ROWS : (zv + 1) * ROWS], 2 * m)
            total = piece if total is None else jnp.where(pair_of == m, piece, total)
        return total

    def columns_of(value):
        return [value[:, j * LANES : (j + 1) * LANES] for j in range(columns)]

    def in_pairs(packed, low, high):
        for k in range(slots // 2):
            second = roll(packed[2 * k + 1], 1)
            low[k] = jnp.where(even, packed[2 * k], second)
            high[k] = jnp.where(even, second, packed[2 * k])

    def first_faces():
        for h in (part, rest):
            packed = []
            for tile in range(slots):
                value = field[0, core, tile] if h is part else extra[tile]
                packed.append(pack(columns_of(value)))
                z_first_low[h, tile : tile + 1, :] = value[:1]
                z_first_high[h, tile : tile + 1, :] = value[half - 1 :]
                if h is part:
                    y_here[core, tile] = packed[tile]
            in_pairs(packed, y_first_low.at[h], y_first_high.at[h])

    def other_faces(tile, carry):
        y_here[other, tile] = pack(columns_of(field[0, other, tile]))
        return carry

    def own_planes():
        @pl.when(part == 0)
        def _():
            z_plus[0][core] = z_first_low[1]

        @pl.when(part == 1)
        def _():
            z_minus[0][core] = z_first_high[0]

    zero = jnp.float32(0.0)
    row = lax.broadcasted_iota(jnp.int32, (half, LANES), 0)

    def entry(tile, k):
        value = nbr[tile, k]
        safe = jnp.maximum(value, 0)
        return value >= 0, lax.rem(safe, slots), safe // slots == block

    def make_weights():
        source = lax.broadcasted_iota(jnp.int32, (2 * LANES, 2 * LANES), 0)
        target = lax.broadcasted_iota(jnp.int32, (2 * LANES, 2 * LANES), 1)
        apart = jnp.abs(source - target)
        same = source // EY == target // EY
        near = jnp.logical_or(apart == EY, jnp.logical_and(apart == 1, same))
        inside = jnp.where(near, 1.0, 0.0).astype(jnp.bfloat16)
        source = lax.broadcasted_iota(jnp.int32, (LANES, 2 * LANES), 0)
        target = lax.broadcasted_iota(jnp.int32, (LANES, 2 * LANES), 1)
        after = jnp.logical_and(source < EY, target == source + 2 * LANES - EY)
        before = jnp.logical_and(source >= LANES - EY, target == source - LANES + EY)
        beside = jnp.where(jnp.logical_or(after, before), 1.0, 0.0).astype(jnp.bfloat16)
        weights[: 2 * LANES, :] = inside
        weights[2 * LANES : 4 * LANES, :] = inside
        weights[4 * LANES : 5 * LANES, :] = beside
        weights[5 * LANES :, :] = beside

    def halves(value):
        high = value.astype(jnp.bfloat16)
        return high, (value - high.astype(jnp.float32)).astype(jnp.bfloat16)

    blocks = columns // 2

    def inner(step, tile, keep_faces):
        now, later = step % 2, (step + 1) % 2
        filled = tile < counts[0]
        left_ok, left, _ = entry(tile, 0)
        right_ok, right, _ = entry(tile, 1)
        fields, lefts = [], []
        for species in range(2):
            parts = columns_of(field[now, species, tile])
            if step == 0:
                parts = [jnp.where(filled, part, zero) for part in parts]
            fields.append(parts)
            ends = [
                jnp.where(left_ok, field[now, species, left, :, cells - LANES :], zero)
            ] + parts + [
                jnp.where(right_ok, field[now, species, right, :, :LANES], zero)
            ]
            split = [halves(part) for part in parts]
            for b in range(blocks):
                beside = halves(jnp.where(below_32, ends[2 * b + 3], ends[2 * b]))
                lefts.append(jnp.concatenate([
                    split[2 * b][0], split[2 * b + 1][0], split[2 * b][1], split[2 * b + 1][1],
                    beside[0], beside[1]], axis=1))
        sums = jnp.dot(
            jnp.concatenate(lefts, axis=0), weights[...], preferred_element_type=jnp.float32)
        amount = columns_of(dens[tile])
        share = [
            amount[j].astype(jnp.float32) / (1.0 + fields[0][j] + fields[1][j])
            for j in range(columns)
        ]
        blank = jnp.zeros((1, LANES), jnp.float32)
        for species in range(2):
            parts = fields[species]
            rate = diffusion[species]
            keep = 1.0 - 6.0 * rate
            taken = uptake[species] * 0.125
            values = []
            for j in range(columns):
                part = parts[j]
                at = (species * blocks + j // 2) * half
                value = sums[at : at + half, (j % 2) * LANES : (j % 2 + 1) * LANES]
                value = value + jnp.concatenate([blank, part[: half - 1]], axis=0)
                value = value + jnp.concatenate([part[1:], blank], axis=0)
                value = part * (keep - taken * share[j]) + rate * value
                field[later, species, tile, :, j * LANES : (j + 1) * LANES] = value
                values.append(value)
            if keep_faces:
                y_part[species, tile] = pack(values)

    top = (half // ROWS - 1) * columns
    sub = lax.broadcasted_iota(jnp.int32, (ROWS, LANES), 0)
    in_low = jnp.logical_and(sub == 0, pair_of < columns)
    in_high = jnp.logical_and(sub == ROWS - 1, pair_of >= top)
    first_row = sub == 0
    last_row = sub == ROWS - 1
    row_pair = lax.rem(lax.broadcasted_iota(jnp.int32, (slots, LANES), 1) + 1, EY) // 2
    row_edge = row_pair == 0

    def pick(ok, ref, *at):
        return jnp.where(ok, ref[at], zero)

    def ghost_of(rate, from_front, from_back, shift):
        return rate * jnp.where(
            even, roll(from_front, 1 - EY - shift), roll(from_back, EY - 1 - shift)
        )

    def paired_ghost(rate, front, back):
        sides = []
        for (ok, slot, here, own, other_block), shift in ((front, 1 - EY), (back, EY - 1)):
            base = jnp.where(ok, jnp.where(here, own, other_block), zero)
            second = jnp.logical_and(jnp.logical_not(here), lax.rem(slot, 2) == 1)
            sides.append(jnp.where(second, roll(base, shift - 1), roll(base, shift)))
        return rate * jnp.where(even, sides[0], sides[1])

    def compact(step):
        into = DONE[step + 1]
        later = (step + 1) % 2
        first = part == 0
        for tile in range(slots):
            filled = tile < counts[0]
            front_ok, front, front_here = entry(tile, 2)
            back_ok, back, back_here = entry(tile, 3)
            lower_ok, lower, _ = entry(tile, 4)
            upper_ok, upper, _ = entry(tile, 5)
            lower = jnp.where(first, lower, tile)
            lower_ok = jnp.where(first, lower_ok, filled)
            upper = jnp.where(first, tile, upper)
            upper_ok = jnp.where(first, filled, upper_ok)
            for species in range(2):
                rate = diffusion[species]
                if step == 1:
                    shift = species
                    from_front = jnp.where(front_here, y_high[step, front], y_minus[step][front])
                    from_back = jnp.where(back_here, y_low[step, back], y_plus[step][back])
                elif step == 2:
                    shift = species
                    from_front = jnp.where(
                        front_here, y_high[DONE[step], front], y_minus[step][front] + g_front[tile])
                    from_back = jnp.where(
                        back_here, y_low[DONE[step], back], y_plus[step][back] + g_back[tile])
                if step == 0:
                    y_ghost[species, tile] = paired_ghost(
                        rate,
                        (front_ok, front, front_here, y_here[species, front],
                         y_minus[0][species, front // 2]),
                        (back_ok, back, back_here, y_here[species, back],
                         y_plus[0][species, back // 2]))
                else:
                    from_front = jnp.where(front_ok, from_front, zero)
                    from_back = jnp.where(back_ok, from_back, zero)
                    y_ghost[species, tile] = ghost_of(rate, from_front, from_back, shift)
                at = slice(tile, tile + 1)
                if step < 2:
                    below = pick(lower_ok, z_minus[step], species, pl.ds(lower, 1), slice(None))
                    above = pick(upper_ok, z_plus[step], species, pl.ds(upper, 1), slice(None))
                else:
                    below = z_minus[step][species, pl.ds(lower, 1), :] + g_below[species, at, :]
                    above = z_plus[step][species, pl.ds(upper, 1), :] + g_above[species, at, :]
                    below = jnp.where(lower_ok, below, zero)
                    above = jnp.where(upper_ok, above, zero)
                below = rate * below
                above = rate * above
                z_ghost_low[species, at, :] = below
                z_ghost_high[species, at, :] = above
                if step != 1:
                    z_low[into, species, at, :] = field[later, species, tile, :1, :] + below
                    z_high[into, species, at, :] = (
                        field[later, species, tile, half - 1 :, :] + above)
        packed = []
        for species in range(2):
            ghosts = [y_ghost[species, tile] for tile in range(slots)]
            edge_low = jnp.concatenate([ghost[:1] for ghost in ghosts], axis=0)
            edge_high = jnp.concatenate([ghost[ROWS - 1 :] for ghost in ghosts], axis=0)
            pack_low = jnp.zeros((slots, LANES), jnp.float32)
            pack_high = jnp.zeros((slots, LANES), jnp.float32)
            for j in range(columns):
                at = slice(j * LANES, (j + 1) * LANES)
                low = roll(z_ghost_low[species, :, at], 2 * j)
                high = roll(z_ghost_high[species, :, at], 2 * (top + j))
                pack_low = jnp.where(row_pair == j, low, pack_low)
                pack_high = jnp.where(row_pair == top + j, high, pack_high)
                if step != 1:
                    z_low[into, species, :, at] += jnp.where(
                        row_edge, roll(edge_low, -2 * j), zero)
                    z_high[into, species, :, at] += jnp.where(
                        row_edge, roll(edge_high, -2 * (top + j)), zero)
            packed.append([
                y_part[species, tile] + ghosts[tile]
                + jnp.where(in_low, jnp.broadcast_to(pack_low[tile : tile + 1], (ROWS, LANES)), zero)
                + jnp.where(in_high, jnp.broadcast_to(pack_high[tile : tile + 1], (ROWS, LANES)), zero)
                for tile in range(slots)
            ])
        if step + 1 == STEPS - 1:
            for species in range(2):
                for tile in range(slots):
                    y_last[species, tile] = packed[species][tile]
                in_pairs(packed[species], y_last_low.at[species], y_last_high.at[species])
        else:
            for tile in range(slots):
                second = roll(packed[1][tile], 1)
                y_low[into, tile] = jnp.where(even, packed[0][tile], second)
                y_high[into, tile] = jnp.where(even, second, packed[0][tile])

    lines = lax.broadcasted_iota(jnp.int32, (slots, LANES), 1)
    line_even = lax.rem(lines, 2) == 0
    in_low_format = lax.rem(lane, EY) // 2

    def rows_of(rows):
        return jnp.concatenate(rows, axis=0)

    def line_ghost(rate, from_front, from_back, shift):
        return rate * jnp.where(
            line_even, roll(from_front, 1 - EY - shift), roll(from_back, EY - 1 - shift)
        )

    def line_copy(source, target, k, device):
        return pltpu.make_async_remote_copy(
            src_ref=source, dst_ref=target, send_sem=line_send.at[k], recv_sem=line_recv.at[k],
            device_id=device, device_id_type=MESH,
        )

    def line_messages():
        both = jnp.logical_and
        out_and_in = [
            (has_plus, has_minus, line_high, near_front, {"row": band + 1}),
            (has_minus, has_plus, line_low, near_back, {"row": band - 1}),
            (both(has_plus, has_far), both(has_minus, has_far), solved_high, far_front,
             {"row": band + 1, "cube": far_layer}),
            (both(has_minus, has_far), both(has_plus, has_far), solved_low, far_back,
             {"row": band - 1, "cube": far_layer}),
        ]
        return [
            (sent, received, line_copy(source, target, k, device))
            for k, (sent, received, source, target, device) in enumerate(out_and_in)
        ]

    def make_lines():
        for tile in range(slots):
            at = slice(tile, tile + 1)
            high, low = y_high[1, tile], y_low[1, tile]
            line_high[at, :] = jnp.where(pair_of[:1] < columns, high[:1], high[ROWS - 1 :])
            line_low[at, :] = jnp.where(in_low_format[:1] < columns, low[:1], low[ROWS - 1 :])
        for k, column in ((0, None), (1, 3)):
            solve(line_high, solved_high, k, column)
        for k, column in ((0, None), (1, 2)):
            solve(line_low, solved_low, k, column)

    def solve(line, solved, k, column):
        names = []
        for tile in range(slots):
            if column is None:
                value = jnp.where(part == 0, nbr[tile, 4], nbr[tile, 5])
                names.append(jnp.where(value >= 0, lax.rem(jnp.maximum(value, 0), slots), -1))
            else:
                ok, slot, here = entry(tile, column)
                names.append(jnp.where(jnp.logical_and(ok, jnp.logical_not(here)), slot, -1))
        found = lax.broadcasted_iota(jnp.int32, (slots, LANES), 0)
        total = jnp.zeros((slots, LANES), jnp.float32)
        for tile in range(slots):
            row = jnp.broadcast_to(line[tile : tile + 1, :], (slots, LANES))
            total = total + jnp.where(found == names[tile], row, zero)
        solved[k] = total

    def partial_faces(step):
        later = (step + 1) % 2
        into = step + 1
        fronts, backs = [], []
        for tile in range(slots):
            second = roll(y_part[1, tile], 1)
            y_low[into, tile] = jnp.where(even, y_part[0, tile], second)
            y_high[into, tile] = jnp.where(even, second, y_part[0, tile])
            front_ok, front, front_here = entry(tile, 2)
            back_ok, back, back_here = entry(tile, 3)
            both = jnp.logical_and
            fronts.append(pick(both(front_ok, front_here), line_high, pl.ds(front, 1), slice(None)))
            backs.append(pick(both(back_ok, back_here), line_low, pl.ds(back, 1), slice(None)))
            for species in range(2):
                at = slice(tile, tile + 1)
                z_low[into, species, at, :] = field[later, species, tile, :1, :]
                z_high[into, species, at, :] = field[later, species, tile, half - 1 :, :]
        fronts, backs = rows_of(fronts), rows_of(backs)
        for species in range(2):
            edge = line_ghost(diffusion[species], fronts, backs, species)
            for j in range(columns):
                at = slice(j * LANES, (j + 1) * LANES)
                z_low[into, species, :, at] += jnp.where(row_edge, roll(edge, -2 * j), zero)
                z_high[into, species, :, at] += jnp.where(
                    row_edge, roll(edge, -2 * (top + j)), zero)

    def own_terms(step):
        low_even_rate = jnp.where(even, diffusion[0], diffusion[1])
        high_even_rate = jnp.where(even, diffusion[1], diffusion[0])
        for tile in range(slots):
            g_front[tile] = high_even_rate * roll(y_low[step, tile], EY - 1)
            g_back[tile] = low_even_rate * roll(y_high[step, tile], 1 - EY)
        for species in range(2):
            g_below[species] = diffusion[species] * z_low[step, species]
            g_above[species] = diffusion[species] * z_high[step, species]

    def complete(step):
        first = part == 0
        both = jnp.logical_and
        every = slice(None)
        shift = 2 * top
        low_even_rate = jnp.where(even, diffusion[0], diffusion[1])
        high_even_rate = jnp.where(even, diffusion[1], diffusion[0])
        below_front, below_back, above_front, above_back = [], [], [], []
        for tile in range(slots):
            front_ok, front, front_here = entry(tile, 2)
            back_ok, back, back_here = entry(tile, 3)
            lower_ok, lower, _ = entry(tile, 4)
            upper_ok, upper, _ = entry(tile, 5)
            far = jnp.where(first, lower, upper)
            far_ok = jnp.where(first, lower_ok, upper_ok)
            front_cross = both(front_ok, jnp.logical_not(front_here))
            back_cross = both(back_ok, jnp.logical_not(back_here))
            near_f = pick(front_cross, near_front, pl.ds(front, 1), every)
            near_b = pick(back_cross, near_back, pl.ds(back, 1), every)
            side_f = pick(both(front_cross, has_far), far_front, 0, pl.ds(front, 1), every)
            side_b = pick(both(back_cross, has_far), far_back, 0, pl.ds(back, 1), every)
            far_f = pick(both(far_ok, has_minus), far_front, 1, pl.ds(far, 1), every)
            far_b = pick(both(far_ok, has_plus), far_back, 1, pl.ds(far, 1), every)
            below_front.append(jnp.where(first, far_f, near_f))
            above_front.append(jnp.where(first, near_f, far_f))
            below_back.append(jnp.where(first, far_b, near_b))
            above_back.append(jnp.where(first, near_b, far_b))

            def placed(near, side, form):
                low = roll(jnp.broadcast_to(jnp.where(first, side, near), (ROWS, LANES)), -shift)
                high = roll(jnp.broadcast_to(jnp.where(first, near, side), (ROWS, LANES)), shift)
                low = jnp.where(both(sub == 0, form < columns), low, zero)
                return low + jnp.where(both(sub == ROWS - 1, form >= top), high, zero)

            g_front[tile] += high_even_rate * placed(near_f, side_f, pair_of)
            g_back[tile] += low_even_rate * placed(near_b, side_b, in_low_format)
        below_front, below_back = rows_of(below_front), rows_of(below_back)
        above_front, above_back = rows_of(above_front), rows_of(above_back)
        for species in range(2):
            below = line_ghost(diffusion[species], below_front, below_back, species)
            above = line_ghost(diffusion[species], above_front, above_back, species)
            for j in range(columns):
                at = slice(j * LANES, (j + 1) * LANES)
                g_below[species, :, at] += jnp.where(
                    row_edge, roll(below, -2 * (top + j)), zero)
                g_above[species, :, at] += jnp.where(row_edge, roll(above, -2 * j), zero)

    def inner_step(step):
        for tile in range(slots):
            inner(step, tile, step < STEPS - 1)
            if step == STEPS - 1:
                give(tile).start()

    def completed(value, ghost, below, above, j):
        pieces = []
        for zv in range(half // ROWS):
            piece = value[zv * ROWS : (zv + 1) * ROWS]
            piece = piece + jnp.where(at_edge[:ROWS], roll(ghost, -2 * (zv * columns + j)), zero)
            if zv == 0:
                piece = piece + jnp.where(first_row, below, zero)
            if zv == half // ROWS - 1:
                piece = piece + jnp.where(last_row, above, zero)
            pieces.append(piece)
        return jnp.concatenate(pieces, axis=0)

    def outer_step(step):
        later = (step + 1) % 2
        for tile in range(slots):
            for species in range(2):
                ghost = y_ghost[species, tile]
                for j in range(columns):
                    at = slice(j * LANES, (j + 1) * LANES)
                    field[later, species, tile, :, at] = completed(
                        field[later, species, tile, :, at], ghost,
                        z_ghost_low[species, tile : tile + 1, at],
                        z_ghost_high[species, tile : tile + 1, at], j)

    def give(tile):
        return pltpu.make_async_remote_copy(
            src_ref=field.at[STEPS % 2, other, tile], dst_ref=out.at[0, tile, own_rows, :],
            send_sem=out_send.at[tile], recv_sem=out_recv.at[tile],
            device_id=partner_id, device_id_type=MESH,
        )

    def take(tile):
        return pltpu.make_async_remote_copy(
            src_ref=field.at[STEPS % 2, other, tile], dst_ref=out.at[0, tile, other_rows, :],
            send_sem=out_send.at[tile], recv_sem=out_recv.at[tile],
            device_id=partner_id, device_id_type=MESH,
        )

    def last_copy(source, target, k, at, device):
        return pltpu.make_async_remote_copy(
            src_ref=source, dst_ref=target,
            send_sem=last_send.at[k], recv_sem=last_recv.at[at],
            device_id=device, device_id_type=MESH,
        )

    def last_sends():
        end = STEPS - 1
        both = jnp.logical_and
        result = []
        for s in range(2):
            target = core * 0 + s
            result += [
                (has_plus, last_copy(
                    y_last_high.at[s], y_last_minus.at[part], 2 + s, 2 + part,
                    {"row": band + 1, "pair": target})),
                (has_minus, last_copy(
                    y_last_low.at[s], y_last_plus.at[part], 4 + s, 4 + part,
                    {"row": band - 1, "pair": target})),
            ]
        for s in range(2):
            target = core * 0 + s
            result += [
                (both(part == 0, has_down), last_copy(
                    z_low.at[end, s], z_last_plus, s, 0, {"cube": layer - 1, "pair": target})),
                (both(part == 1, has_up), last_copy(
                    z_high.at[end, s], z_last_minus, s, 1, {"cube": layer + 1, "pair": target})),
            ]
        return result + [
            (always, last_copy(y_last.at[other], y_last_here, 6, 6, partner_id)),
            (part == 0, last_copy(z_high.at[end, other], z_near, 7, 7, partner_id)),
            (part == 1, last_copy(z_low.at[end, other], z_near, 7, 7, partner_id)),
        ]

    def last_receives():
        arrivals = [(has_up, z_last_plus, 0), (has_down, z_last_minus, 1)]
        for h in range(2):
            arrivals.append((has_minus, y_last_minus.at[h], 2 + h))
            arrivals.append((has_plus, y_last_plus.at[h], 4 + h))
        arrivals += [(always, y_last_here, 6), (always, z_near, 7)]
        return [(wanted, last_copy(ref, ref, 0, at, partner_id)) for wanted, ref, at in arrivals]

    def last_step():
        rate = diffusion[core]
        first = part == 0
        end = STEPS - 1
        every = slice(None)
        for tile in range(slots):
            front_ok, front, front_here = entry(tile, 2)
            back_ok, back, back_here = entry(tile, 3)
            lower_ok, lower, _ = entry(tile, 4)
            upper_ok, upper, _ = entry(tile, 5)
            at = slice(tile, tile + 1)
            bottom = pick(lower_ok, z_last_minus, pl.ds(lower, 1), every)
            ceiling = pick(upper_ok, z_last_plus, pl.ds(upper, 1), every)
            near = z_near[at, :]
            mine = jnp.where(first, z_high[end, core, at, :], z_low[end, core, at, :])
            for h, rows in ((part, own_rows), (rest, other_rows)):
                if h is part:
                    front_in, back_in = y_last[core, front], y_last[core, back]
                    below = rate * jnp.where(first, bottom, near)
                    above = rate * jnp.where(first, near, ceiling)
                else:
                    front_in, back_in = y_last_here[front], y_last_here[back]
                    below = rate * jnp.where(first, mine, bottom)
                    above = rate * jnp.where(first, ceiling, mine)
                ghost = paired_ghost(
                    rate,
                    (front_ok, front, front_here, front_in, y_last_minus[h, front // 2]),
                    (back_ok, back, back_here, back_in, y_last_plus[h, back // 2]))
                for j in range(columns):
                    lanes = slice(j * LANES, (j + 1) * LANES)
                    if h is part:
                        value = field[STEPS % 2, core, tile, :, lanes]
                    else:
                        value = out[0, tile, rows, lanes]
                    out[0, tile, rows, lanes] = completed(
                        value, ghost, below[:, lanes], above[:, lanes], j)

    loads[0].wait()
    loads[1].wait()
    make_weights()
    first_faces()
    pl.semaphore_wait(barrier, peers)
    for wanted, copy in first_sends():
        pl.when(wanted)(copy.start)
    swap.start()
    own_planes()
    for load in smalls:
        load.wait()
    loads[2].wait()
    swap_in.wait_recv()
    lax.fori_loop(0, slots, other_faces, 0, unroll=True)
    inner_step(0)
    wait_first()
    compact(0)
    make_lines()
    for sent, _, copy in line_messages()[::-1]:
        pl.when(sent)(copy.start)
    send_faces(1)
    outer_step(0)
    inner_step(1)
    partial_faces(1)
    send_faces(2)
    own_terms(1)
    wait_faces(1)
    compact(1)
    outer_step(1)
    inner_step(2)
    for _, received, copy in line_messages():
        pl.when(received)(copy.wait_recv)
    complete(1)
    wait_faces(2)
    compact(2)
    for wanted, copy in last_sends():
        pl.when(wanted)(copy.start)
    outer_step(2)
    inner_step(STEPS - 1)
    for tile in range(slots):
        take(tile).wait_recv()
    for wanted, copy in last_receives():
        pl.when(wanted)(copy.wait_recv)
    last_step()
    swap.wait_send()
    for wanted, copy in first_sends():
        pl.when(wanted)(copy.wait_send)
    for step in range(1, STEPS - 1):
        wait_sent(step)
    for sent, _, copy in line_messages():
        pl.when(sent)(copy.wait_send)
    for wanted, copy in last_sends():
        pl.when(wanted)(copy.wait_send)
    for tile in range(slots):
        give(tile).wait_send()


def per_device(layers, bands, ligand, density, counts, neighbours, diffusion, uptake):
    _, slots, depth, cells = ligand.shape
    half = depth // 2
    faces = (slots, ROWS, LANES)
    pairs = (slots // 2, ROWS, LANES)
    planes = (2, slots, cells)
    away = pl.BlockSpec(memory_space=pltpu.HBM)
    neighbours, diffusion, uptake = [
        pltpu.with_memory_space_constraint(x, pltpu.HBM) for x in (neighbours, diffusion, uptake)
    ]
    return pl.pallas_call(
        functools.partial(kernel, layers, bands, slots, half, cells),
        out_shape=jax.ShapeDtypeStruct(ligand.shape, jnp.float32),
        in_specs=[away] * 6,
        out_specs=pl.BlockSpec(memory_space=pltpu.VMEM),
        scratch_shapes=[
            pltpu.VMEM((2, 2, slots, half, cells), jnp.float32),
            pltpu.VMEM((slots, half, cells), jnp.int32),
            pltpu.VMEM((STEPS + 1,) + faces, jnp.float32),
            pltpu.VMEM((STEPS + 1,) + faces, jnp.float32),
            [pltpu.VMEM((2,) + pairs, jnp.float32)] + [pltpu.VMEM(faces, jnp.float32)] * (STEPS - 2),
            [pltpu.VMEM((2,) + pairs, jnp.float32)] + [pltpu.VMEM(faces, jnp.float32)] * (STEPS - 2),
            pltpu.VMEM((STEPS + 1,) + planes, jnp.float32),
            pltpu.VMEM((STEPS + 1,) + planes, jnp.float32),
            [pltpu.VMEM(planes, jnp.float32)] * (STEPS - 1),
            [pltpu.VMEM(planes, jnp.float32)] * (STEPS - 1),
            pltpu.VMEM((slots, half, cells), jnp.float32),
            pltpu.VMEM((2,) + pairs, jnp.float32),
            pltpu.VMEM((2,) + pairs, jnp.float32),
            pltpu.VMEM((2,) + faces, jnp.float32),
            pltpu.VMEM(planes, jnp.float32),
            pltpu.VMEM(planes, jnp.float32),
            pltpu.VMEM((2,) + faces, jnp.float32),
            pltpu.VMEM((2,) + faces, jnp.float32),
            pltpu.VMEM(planes, jnp.float32),
            pltpu.VMEM(planes, jnp.float32),
            pltpu.VMEM((2,) + faces, jnp.float32),
            pltpu.VMEM((2,) + pairs, jnp.float32),
            pltpu.VMEM((2,) + pairs, jnp.float32),
            pltpu.VMEM(faces, jnp.float32),
            pltpu.VMEM((2,) + pairs, jnp.float32),
            pltpu.VMEM((2,) + pairs, jnp.float32),
            pltpu.VMEM((slots, cells), jnp.float32),
            pltpu.VMEM((slots, cells), jnp.float32),
            pltpu.VMEM((slots, cells), jnp.float32),
            pltpu.VMEM((slots, LANES), jnp.float32),
            pltpu.VMEM((slots, LANES), jnp.float32),
            pltpu.VMEM((2, slots, LANES), jnp.float32),
            pltpu.VMEM((2, slots, LANES), jnp.float32),
            pltpu.VMEM((slots, LANES), jnp.float32),
            pltpu.VMEM((slots, LANES), jnp.float32),
            pltpu.VMEM((2, slots, LANES), jnp.float32),
            pltpu.VMEM((2, slots, LANES), jnp.float32),
            pltpu.VMEM(faces, jnp.float32),
            pltpu.VMEM(faces, jnp.float32),
            pltpu.VMEM(planes, jnp.float32),
            pltpu.VMEM(planes, jnp.float32),
            pltpu.VMEM((6 * LANES, 2 * LANES), jnp.bfloat16),
            pltpu.SMEM((slots, 6), jnp.int32),
            pltpu.SMEM((1,), jnp.int32),
            pltpu.SMEM((2,), jnp.float32),
            pltpu.SMEM((2,), jnp.float32),
            pltpu.SemaphoreType.DMA((8,)),
            pltpu.SemaphoreType.DMA((4, 2)),
            pltpu.SemaphoreType.DMA((3,)),
            pltpu.SemaphoreType.DMA((4,)),
            pltpu.SemaphoreType.DMA,
            pltpu.SemaphoreType.DMA,
            pltpu.SemaphoreType.DMA((STEPS, 4)),
            pltpu.SemaphoreType.DMA((STEPS, 4)),
            pltpu.SemaphoreType.DMA((4,)),
            pltpu.SemaphoreType.DMA((4,)),
            pltpu.SemaphoreType.DMA((8,)),
            pltpu.SemaphoreType.DMA((8,)),
            pltpu.SemaphoreType.DMA((slots,)),
            pltpu.SemaphoreType.DMA((slots,)),
        ],
        compiler_params=pltpu.CompilerParams(
            collective_id=0, has_side_effects=True, vmem_limit_bytes=53 * 1024 * 1024
        ),
    )(neighbours, counts, diffusion, uptake, ligand, density)


def solution(mesh):
    in_specs = (
        P("pair", ("groups", "cube", "row"), None, None),
        P(("groups", "cube", "row"), None, None),
        P(("groups", "cube", "row")),
        P(("groups", "cube", "row"), None),
        P(),
        P(),
    )
    out_specs = P("pair", ("groups", "cube", "row"), None, None)
    return jax.shard_map(
        functools.partial(per_device, mesh.shape["cube"], mesh.shape["row"]),
        mesh=mesh, in_specs=in_specs, out_specs=out_specs, check_vma=False,
    )
```
